32 devices in a mesh: seq: 8 (over z, x), fsdp: 4 (over y, core).
Axes of the slice: x: 2, y: 2, z: 4, core: 2. Of those that a mesh axis runs over, the one named last changes fastest.
Arguments:
- block_input: bfloat16 [8, 1024, 1536], P('fsdp', 'seq'), may hold values from -6 to 6
- dilated_weight: bfloat16 [3, 1536, 768], P(None, 'fsdp'), may hold values from -0.09375 to 0.09375
- w_project: bfloat16 [768, 1536], P('fsdp'), may hold values from -0.21875 to 0.21875
- gain_first: float32 [1536], replicated, may hold values from 0.5 to 1.5
- gain_second: float32 [768], replicated, may hold values from 0.5 to 1.5
- grad_output: bfloat16 [8, 1024, 1536], P('fsdp', 'seq'), may hold values from -6 to 6
Outputs:
- grad_input: bfloat16 [8, 1024, 1536], P('fsdp', 'seq')
- grad_gain_first: float32 [1536], replicated
- grad_gain_second: float32 [768], replicated
The draws below stay inside these ranges and needn't reach their ends.
All inputs are finite; a program needn't handle non-finite values.
Results may differ from the reference program's by a relative error of at most 0.008.
Values may be sent and summed in bfloat16 or wider, within the bound.
A program may use at most 64 MiB of HBM per device.

```python
import jax
import jax.numpy as jnp
from jax import lax

C = 1536
H = 768
BATCH = 8
BINS = 1024
DILATION_STEP = 128


def steps_of(own_key, dims, cuts, least, top_value):
    factor_of, own = 1.0, jax.random.fold_in(own_key, 6)
    for dim, blocks in cuts:
        heights = jnp.exp(jax.random.uniform(jax.random.fold_in(own, dim), (blocks,), jnp.float32, least / len(cuts), top_value / len(cuts)))
        factor_of = factor_of * jnp.repeat(heights, dims[dim] // blocks).reshape([-1 if axis == dim else 1 for axis in range(len(dims))])
    return factor_of


def noise(key, shape, deviation, bound, shards=(), held_as=jnp.bfloat16):
    values = jax.random.normal(key, shape, jnp.float32) * deviation
    if len(shards) > 0:
        values = steps_of(key, shape, shards, -0.22, 0.18) * values
    return jnp.clip(values, min=-bound, max=bound).astype(held_as)


def setup_inputs(seed: int = 0) -> dict:
    keys = jax.random.split(jax.random.key(seed), 7)
    return {
        "block_input": noise(keys[0], (BATCH, BINS, C), 1.0, 6.0, ((0, 4), (1, 8))),
        "dilated_weight": noise(keys[1], (3, C, H), (3 * C) ** -0.5, 0.09375, ((1, 4),)),
        "w_project": noise(keys[2], (H, C), H ** -0.5, 0.21875, ((0, 4),)),
        "gain_first": jnp.clip(1.0 + 0.1 * jax.random.normal(keys[3], (C,), jnp.float32), 0.5, 1.5),
        "gain_second": jnp.clip(1.0 + 0.1 * jax.random.normal(keys[4], (H,), jnp.float32), 0.5, 1.5),
        "grad_output": noise(keys[5], (BATCH, BINS, C), 1.0, 6.0, ((0, 4), (1, 8))),
    }


def norm_act(values, factor):
    centre = values - lax.optimization_barrier(jnp.mean(values, axis=-1, keepdims=True))
    spread = lax.optimization_barrier(jnp.mean(centre * centre, axis=-1, keepdims=True))
    return jax.nn.gelu(centre * lax.rsqrt(spread + 1e-05) * factor)

def displace_rows(values, amount):
    if amount > 0:
        return jnp.concatenate([jnp.zeros_like(values[:amount]), values[:-amount]], axis=0)
    return jnp.concatenate([values[-amount:], jnp.zeros_like(values[:-amount])], axis=0)

def reference(block_input, dilated_weight, w_project, gain_first, gain_second, grad_output):

    def per_sample(sample):
        inputs, cotangent = sample
        widened = inputs.astype(jnp.float32)
        hidden_state = norm_act(widened, gain_first).astype(jnp.bfloat16)
        mixed_state = jnp.dot(displace_rows(hidden_state, DILATION_STEP), dilated_weight[0], preferred_element_type=jnp.float32)
        mixed_state = mixed_state + jnp.dot(hidden_state, dilated_weight[1], preferred_element_type=jnp.float32)
        mixed_state = mixed_state + jnp.dot(displace_rows(hidden_state, -DILATION_STEP), dilated_weight[2], preferred_element_type=jnp.float32)
        mixed_state = mixed_state.astype(jnp.bfloat16)
        grad_hidden2 = jnp.dot(cotangent, w_project.T, preferred_element_type=jnp.float32)
        unused, pull_second = jax.vjp(norm_act, mixed_state.astype(jnp.float32), gain_second)
        mixed_gradient, grad_second = pull_second(grad_hidden2)
        mixed_gradient = mixed_gradient.astype(jnp.bfloat16)
        hidden_gradient = jnp.dot(displace_rows(mixed_gradient, -DILATION_STEP), dilated_weight[0].T, preferred_element_type=jnp.float32)
        hidden_gradient = hidden_gradient + jnp.dot(mixed_gradient, dilated_weight[1].T, preferred_element_type=jnp.float32)
        hidden_gradient = hidden_gradient + jnp.dot(displace_rows(mixed_gradient, DILATION_STEP), dilated_weight[2].T, preferred_element_type=jnp.float32)
        unused2, pull_first = jax.vjp(norm_act, widened, gain_first)
        grad_branch, grad_first = pull_first(hidden_gradient)
        grad_in = (cotangent.astype(jnp.float32) + grad_branch).astype(jnp.bfloat16)
        return (grad_in, grad_first, grad_second)
    grad_input, first_terms, second_terms = lax.map(per_sample, (block_input, grad_output))
    return (grad_input, lax.optimization_barrier(jnp.sum(first_terms, axis=0)), lax.optimization_barrier(jnp.sum(second_terms, axis=0)))
```

```python
import functools

import jax
import jax.numpy as jnp
from jax import lax
from jax.experimental import pallas as pl
from jax.experimental.pallas import tpu as pltpu
from jax.sharding import PartitionSpec as P

MESH = pl.DeviceIdType.MESH
TAPS = (0, 2, 1)
CHUNKS = 2
UNITS = 4
EPS = 1e-05
K0 = 0.7978845608028654
K1 = 0.044715


def normed(values):
    centre = values - jnp.mean(values, axis=-1, keepdims=True)
    scale = lax.rsqrt(jnp.mean(centre * centre, axis=-1, keepdims=True) + EPS)
    return centre * scale, scale


def gelu_parts(a):
    square = a * a
    t = jnp.tanh(a * (K0 + (K0 * K1) * square))
    half = 0.5 + 0.5 * t
    slope = half + (0.5 * a) * (1.0 - t * t) * (K0 + (3.0 * K0 * K1) * square)
    return a * half, slope


def dot(a, b):
    return jnp.dot(a, b, preferred_element_type=jnp.float32)


def dot_t(a, b):
    return lax.dot_general(a, b, (((1,), (1,)), ((), ())), preferred_element_type=jnp.float32)


def fold(values):
    rows, columns = values.shape
    return jnp.sum(values.reshape(rows // 8, 8, columns), axis=0)


def kernel(
    seqs, x_ref, w_ref, p_ref, g1_ref, g2_ref, go_ref,
    out_ref, sum1_ref, sum2_ref,
    xbuf, gbuf, wbuf, pbuf, hbuf, n1, q1, r1, acc, n2, q2, r2, psend, rfwd, gmx, gh, obuf,
    part1, part2, fslots, sslots,
    y_s, y_r, z_s, z_r, a_s, a_r, b_s, b_r, own_s, own_r, own_l,
    sw_s, sw_r, sw_l, fw_s, fw_r, bw_s, bw_r, o_s, o_r, o_l, gf_s, gf_r, gs_s, gs_r,
):
    bins, chans = xbuf.shape[1], xbuf.shape[2]
    hid = pbuf.shape[0]
    wrows, prows = w_ref.shape[1], p_ref.shape[0]
    s, f = lax.axis_index("seq"), lax.axis_index("fsdp")
    reach = seqs // 8
    block = s // reach
    p, q = block // 2, block % 2
    zp = p % 2
    mate = s + reach - 2 * reach * q
    zmate = s + 2 * reach - 4 * reach * zp
    nxt, prv = s + 2 * reach, s - 2 * reach
    sib = f + 1 - 2 * (f % 2)
    far = (f + 2) % 4
    far_sib = (sib + 2) % 4

    def rc(src, dst, ss, rs, seq, fs):
        return pltpu.make_async_remote_copy(
            src_ref=src, dst_ref=dst, send_sem=ss, recv_sem=rs,
            device_id=(seq, fs), device_id_type=MESH,
        )

    barrier = pltpu.get_barrier_semaphore()

    def greet(i, carry):
        pl.semaphore_signal(barrier, inc=1, device_id=((s + i) % seqs, f), device_id_type=MESH)
        return carry

    lax.fori_loop(1, seqs, greet, 0)
    for i in range(1, 4):
        pl.semaphore_signal(barrier, inc=1, device_id=(s, (f + i) % 4), device_id_type=MESH)
    pl.semaphore_wait(barrier, seqs - 1 + 3)

    def held(u, owner, half, c):
        if u < 3:
            n = wrows // 2 // CHUNKS
            at = pl.multiple_of(owner * wrows + half * (wrows // 2) + c * n, 16)
            return wbuf.at[TAPS[u], pl.ds(at, n)]
        n = prows // 2 // CHUNKS
        at = pl.multiple_of(owner * prows + half * (prows // 2) + c * n, 16)
        return pbuf.at[pl.ds(at, n)]

    def mine(u, half, c):
        if u < 3:
            n = wrows // 2 // CHUNKS
            return w_ref.at[TAPS[u], pl.ds(pl.multiple_of(half * (wrows // 2) + c * n, 16), n)]
        n = prows // 2 // CHUNKS
        return p_ref.at[pl.ds(pl.multiple_of(half * (prows // 2) + c * n, 16), n)]

    def held_unit(u, owner):
        if u < 3:
            return wbuf.at[TAPS[u], pl.ds(pl.multiple_of(owner * wrows, 16), wrows)]
        return pbuf.at[pl.ds(pl.multiple_of(owner * prows, 16), prows)]

    def my_unit(u):
        return w_ref.at[TAPS[u]] if u < 3 else p_ref

    def y_copy(j, owner):
        u, c = j // CHUNKS, j % CHUNKS
        return rc(mine(u, zp, c), held(u, owner, zp, c), y_s.at[j], y_r.at[j], s, far)

    def z_copy(j, half):
        piece = held(j // CHUNKS, far, half, j % CHUNKS)
        return rc(piece, piece, z_s.at[j], z_r.at[j], zmate, f)

    def a_copy(j, owner):
        piece = held(j // CHUNKS, owner, zp, j % CHUNKS)
        return rc(piece, piece, a_s.at[j], a_r.at[j], s, sib)

    def b_copy(j, owner):
        piece = held(j // CHUNKS, owner, 1 - zp, j % CHUNKS)
        return rc(piece, piece, b_s.at[j], b_r.at[j], s, sib)

    def own_copy(u, owner):
        return rc(my_unit(u), held_unit(u, owner), own_s.at[u], own_r.at[u], s, sib)

    def own_local(u):
        return pltpu.make_async_copy(my_unit(u), held_unit(u, f), own_l.at[u])

    def swap(k, slot):
        ref, buf = ((x_ref, xbuf), (go_ref, gbuf))[k]
        return rc(ref.at[1 - q], buf.at[slot], sw_s.at[k], sw_r.at[k], mate, f)

    def swap_local(k):
        ref, buf = ((x_ref, xbuf), (go_ref, gbuf))[k]
        return pltpu.make_async_copy(ref.at[q], buf.at[q], sw_l.at[k])

    steps = UNITS * CHUNKS
    swap_local(0).start()
    swap(0, q).start()
    for j in range(steps):
        y_copy(j, f).start()
    for u in range(UNITS):
        own_copy(u, f).start()
        own_local(u).start()
    swap(1, q).start()
    swap_local(1).start()

    tile = 32
    per = bins // tile

    def first_act(which):
        def go(i, carry):
            at = pl.multiple_of(which * bins + i * tile, tile)
            rows = pl.ds(at, tile)
            v = xbuf[which, pl.ds(pl.multiple_of(i * tile, tile), tile), :].astype(jnp.float32)
            n, scale = normed(v)
            act, slope = gelu_parts(n * g1_ref[...])
            hbuf[rows, :] = act.astype(jnp.bfloat16)
            n1[rows, :] = n
            q1[rows, :] = slope
            r1[rows, :] = jnp.broadcast_to(scale, (tile, 128))
            return carry

        lax.fori_loop(0, per, go, 0)

    def pump(j):
        if j < steps:
            y_copy(j, far).wait_recv()
            z_copy(j, zp).start()
            a_copy(j, far).start()
        if 0 < j <= steps:
            z_copy(j - 1, 1 - zp).wait_recv()
            b_copy(j - 1, far).start()

    def unit_ready(u):
        own_local(u).wait()
        own_copy(u, sib).wait_recv()
        for c in range(CHUNKS):
            a_copy(u * CHUNKS + c, far_sib).wait_recv()
            b_copy(u * CHUNKS + c, far_sib).wait_recv()

    swap_local(0).wait()
    first_act(q)
    pump(0)
    pump(1)
    swap(0, 1 - q).wait_recv()
    first_act(1 - q)
    pump(2)
    unit_ready(0)

    def fwd(k):
        return dot(hbuf[...], wbuf[k])

    tap = fwd(0)
    acc[bins:, :] = tap[:bins, :]
    psend[0] = tap[bins:, :].astype(jnp.bfloat16)
    last = seqs // (2 * reach) - 1

    def to_next(src, dst, ss, rs):
        return rc(src, dst, ss, rs, nxt, f)

    def to_prev(src, dst, ss, rs):
        return rc(src, dst, ss, rs, prv, f)

    fwd_next = to_next(psend.at[0], rfwd.at[0], fw_s.at[0], fw_r.at[0])
    fwd_prev = to_prev(psend.at[1], rfwd.at[1], fw_s.at[1], fw_r.at[1])
    pl.when(p < last)(lambda: fwd_next.start())
    pump(3)
    pump(4)
    unit_ready(1)
    tap = fwd(2)
    acc[:bins, :] = tap[bins:, :]
    psend[1] = tap[:bins, :].astype(jnp.bfloat16)
    pl.when(p > 0)(lambda: fwd_prev.start())
    pump(5)
    pump(6)
    unit_ready(2)
    acc[...] += fwd(1)
    pump(7)

    def zero_first():
        rfwd[0] = jnp.zeros_like(rfwd[0])
        gmx[:bins, :] = jnp.zeros((bins, hid), jnp.bfloat16)

    def zero_last():
        rfwd[1] = jnp.zeros_like(rfwd[1])
        gmx[3 * bins:, :] = jnp.zeros((bins, hid), jnp.bfloat16)

    pl.when(p == 0)(zero_first)
    pl.when(p == last)(zero_last)
    pl.when(p > 0)(lambda: fwd_next.wait_recv())
    pl.when(p < last)(lambda: fwd_prev.wait_recv())

    def second_act(i, carry):
        for which in range(2):
            rows = pl.ds(pl.multiple_of(which * bins + i * tile, tile), tile)
            got = rfwd[which, pl.ds(pl.multiple_of(i * tile, tile), tile), :]
            v = (acc[rows, :] + got.astype(jnp.float32)).astype(jnp.bfloat16).astype(jnp.float32)
            n, scale = normed(v)
            unused, slope = gelu_parts(n * g2_ref[...])
            n2[rows, :] = n
            q2[rows, :] = slope
            r2[rows, :] = jnp.broadcast_to(scale, (tile, 128))
        return carry

    lax.fori_loop(0, per, second_act, 0)
    pump(8)
    swap_local(1).wait()
    swap(1, 1 - q).wait_recv()
    unit_ready(3)
    acc[...] = dot_t(gbuf[...].reshape(2 * bins, chans), pbuf[...])

    def back(rows, d, n, slope, r, gain, part):
        da = d * slope
        part[...] += fold(da * n)
        dn = da * gain
        m1 = jnp.mean(dn, axis=-1, keepdims=True)
        m2 = jnp.mean(dn * n, axis=-1, keepdims=True)
        return r[rows, 0:1] * (dn - m1 - n * m2)

    part1[...] = jnp.zeros_like(part1)
    part2[...] = jnp.zeros_like(part2)

    def second_back(i, carry):
        rows = pl.ds(pl.multiple_of(i * tile, tile), tile)
        dv = back(rows, acc[rows, :], n2[rows, :], q2[rows, :], r2, g2_ref[...], part2)
        gmx[pl.ds(pl.multiple_of(bins + i * tile, tile), tile), :] = dv.astype(jnp.bfloat16)
        return carry

    lax.fori_loop(0, 2 * per, second_back, 0)

    bwd_next = to_next(gmx.at[pl.ds(2 * bins, bins)], gmx.at[pl.ds(0, bins)], bw_s.at[0], bw_r.at[0])
    bwd_prev = to_prev(gmx.at[pl.ds(bins, bins)], gmx.at[pl.ds(3 * bins, bins)], bw_s.at[1], bw_r.at[1])
    pl.when(p < last)(lambda: bwd_next.start())
    pl.when(p > 0)(lambda: bwd_prev.start())
    gh[...] = dot_t(gmx[bins:3 * bins, :], wbuf[1])
    pl.when(p > 0)(lambda: bwd_next.wait_recv())
    pl.when(p < last)(lambda: bwd_prev.wait_recv())
    gh[...] += dot_t(gmx[2 * bins:, :], wbuf[0])
    gh[...] += dot_t(gmx[:2 * bins, :], wbuf[2])

    def first_back(which):
        def go(i, carry):
            rows = pl.ds(pl.multiple_of(which * bins + i * tile, tile), tile)
            here = pl.ds(pl.multiple_of(i * tile, tile), tile)
            dv = back(rows, gh[rows, :], n1[rows, :], q1[rows, :], r1, g1_ref[...], part1)
            obuf[which, here, :] = (gbuf[which, here, :].astype(jnp.float32) + dv).astype(jnp.bfloat16)
            return carry

        lax.fori_loop(0, per, go, 0)

    first_back(1 - q)
    out_mate = rc(obuf.at[1 - q], out_ref.at[q], o_s.at[0], o_r.at[0], mate, f)
    out_mate.start()
    first_back(q)
    out_own = pltpu.make_async_copy(obuf.at[q], out_ref.at[q], o_l.at[0])
    out_own.start()

    fslots[f, :, :chans] = jnp.sum(part1[...], axis=0, keepdims=True)
    fslots[f, :, chans:] = jnp.sum(part2[...], axis=0, keepdims=True)

    def f_copy(owner, other):
        return rc(fslots.at[owner], fslots.at[owner], gf_s.at[other], gf_r.at[owner], s, other)

    for i in range(1, 4):
        f_copy(f, (f + i) % 4).start()
    for i in range(1, 4):
        f_copy((f + i) % 4, (f + i) % 4).wait_recv()
    sslots[s] = jnp.sum(fslots[...], axis=0)

    def s_copy(owner, other):
        return rc(sslots.at[owner], sslots.at[owner], gs_s.at[other], gs_r.at[owner], other, f)

    def s_send(i, carry):
        s_copy(s, (s + i) % seqs).start()
        return carry

    def s_recv(i, carry):
        s_copy((s + i) % seqs, (s + i) % seqs).wait_recv()
        return carry

    def s_done(i, carry):
        s_copy(s, (s + i) % seqs).wait_send()
        return carry

    lax.fori_loop(1, seqs, s_send, 0)
    lax.fori_loop(1, seqs, s_recv, 0)
    total = jnp.sum(sslots[...], axis=0)
    sum1_ref[...] = total[:, :chans]
    sum2_ref[...] = total[:, chans:]

    lax.fori_loop(1, seqs, s_done, 0)
    for i in range(1, 4):
        f_copy(f, (f + i) % 4).wait_send()
    for j in range(steps):
        y_copy(j, f).wait_send()
        z_copy(j, zp).wait_send()
        a_copy(j, far).wait_send()
        b_copy(j, far).wait_send()
    for u in range(UNITS):
        own_copy(u, f).wait_send()
    for k in range(2):
        swap(k, q).wait_send()
    pl.when(p < last)(lambda: fwd_next.wait_send())
    pl.when(p > 0)(lambda: fwd_prev.wait_send())
    pl.when(p < last)(lambda: bwd_next.wait_send())
    pl.when(p > 0)(lambda: bwd_prev.wait_send())
    out_own.wait()
    out_mate.wait_send()
    rc(obuf.at[1 - q], out_ref.at[1 - q], o_s.at[0], o_r.at[0], mate, f).wait_recv()


def body(block_input, dilated_weight, w_project, gain_first, gain_second, grad_output):
    seqs = lax.axis_size("seq")
    fsdps = lax.axis_size("fsdp")
    samples, bins, chans = block_input.shape
    hid = w_project.shape[0] * fsdps
    rows = 2 * bins
    bf16, f32 = jnp.bfloat16, jnp.float32
    dma = lambda n: pltpu.SemaphoreType.DMA((n,))
    steps = UNITS * CHUNKS
    anywhere = pl.BlockSpec(memory_space=pl.ANY)
    vmem = pl.BlockSpec(memory_space=pltpu.VMEM)
    out, sum1, sum2 = pl.pallas_call(
        functools.partial(kernel, seqs),
        out_shape=(
            jax.ShapeDtypeStruct(block_input.shape, bf16),
            jax.ShapeDtypeStruct((1, chans), f32),
            jax.ShapeDtypeStruct((1, hid), f32),
        ),
        in_specs=[anywhere, anywhere, anywhere, vmem, vmem, anywhere],
        out_specs=(anywhere, vmem, vmem),
        scratch_shapes=[
            pltpu.VMEM((2, bins, chans), bf16),
            pltpu.VMEM((2, bins, chans), bf16),
            pltpu.VMEM((3, chans, hid), bf16),
            pltpu.VMEM((hid, chans), bf16),
            pltpu.VMEM((rows, chans), bf16),
            pltpu.VMEM((rows, chans), f32),
            pltpu.VMEM((rows, chans), f32),
            pltpu.VMEM((rows, 128), f32),
            pltpu.VMEM((rows, hid), f32),
            pltpu.VMEM((rows, hid), f32),
            pltpu.VMEM((rows, hid), f32),
            pltpu.VMEM((rows, 128), f32),
            pltpu.VMEM((2, bins, hid), bf16),
            pltpu.VMEM((2, bins, hid), bf16),
            pltpu.VMEM((2 * rows, hid), bf16),
            pltpu.VMEM((rows, chans), f32),
            pltpu.VMEM((2, bins, chans), bf16),
            pltpu.VMEM((8, chans), f32),
            pltpu.VMEM((8, hid), f32),
            pltpu.VMEM((fsdps, 1, chans + hid), f32),
            pltpu.VMEM((seqs, 1, chans + hid), f32),
        ]
        + [dma(steps)] * 8
        + [dma(UNITS)] * 3
        + [dma(2)] * 3
        + [dma(2)] * 4
        + [dma(1)] * 3
        + [dma(fsdps)] * 2
        + [dma(seqs)] * 2,
        compiler_params=pltpu.CompilerParams(
            collective_id=0, has_side_effects=True, vmem_limit_bytes=52 * 1024 * 1024
        ),
    )(
        block_input, dilated_weight, w_project,
        gain_first.reshape(1, chans), gain_second.reshape(1, hid), grad_output,
    )
    return out, sum1.reshape(chans), sum2.reshape(hid)


def solution(mesh):
    in_specs = (
        P("fsdp", "seq", None),
        P(None, "fsdp", None),
        P("fsdp", None),
        P(),
        P(),
        P("fsdp", "seq", None),
    )
    out_specs = (P("fsdp", "seq", None), P(), P())
    return jax.shard_map(body, mesh=mesh, in_specs=in_specs, out_specs=out_specs, check_vma=False)
```

```python
import functools

import jax
import jax.numpy as jnp
from jax import lax
from jax.experimental import pallas as pl
from jax.experimental.pallas import tpu as pltpu
from jax.sharding import PartitionSpec as P

MESH = pl.DeviceIdType.MESH
TAPS = (0, 2, 1)
CHUNKS = 3
LAG = 2
AHEAD = 3
UNITS = 4
EPS = 1e-05
K0 = 0.7978845608028654
K1 = 0.044715


def normed(values):
    centre = values - jnp.mean(values, axis=-1, keepdims=True)
    scale = lax.rsqrt(jnp.mean(centre * centre, axis=-1, keepdims=True) + EPS)
    return centre * scale, scale


def gelu_parts(a):
    square = a * a
    t = jnp.tanh(a * (K0 + (K0 * K1) * square))
    half = 0.5 + 0.5 * t
    slope = half + (0.5 * a) * (1.0 - t * t) * (K0 + (3.0 * K0 * K1) * square)
    return a * half, slope


def dot(a, b):
    return jnp.dot(a, b, preferred_element_type=jnp.float32)


def dot_t(a, b):
    return lax.dot_general(a, b, (((1,), (1,)), ((), ())), preferred_element_type=jnp.float32)


def fold(values):
    rows, columns = values.shape
    return jnp.sum(values.reshape(rows // 8, 8, columns), axis=0)


def kernel(
    seqs, x_ref, w_ref, p_ref, g1_ref, g2_ref, go_ref,
    out_ref, sum1_ref, sum2_ref,
    xbuf, gbuf, wbuf, pbuf, hbuf, n1, q1, r1, acc, n2, q2, r2, psend, rfwd, gmx, gh, obuf,
    part1, part2, fslots, sslots,
    y_s, y_r, z_s, z_r, a_s, a_r, b_s, b_r, own_s, own_r, own_l,
    sw_s, sw_r, sw_l, fw_s, fw_r, bw_s, bw_r, o_s, o_r, o_l, gf_s, gf_r, gs_s, gs_r,
):
    bins, chans = xbuf.shape[1], xbuf.shape[2]
    hid = pbuf.shape[0]
    wrows, prows = w_ref.shape[1], p_ref.shape[0]
    s, f = lax.axis_index("seq"), lax.axis_index("fsdp")
    reach = seqs // 8
    block = s // reach
    p, q = block // 2, block % 2
    zp = p % 2
    mate = s + reach - 2 * reach * q
    zmate = s + 2 * reach - 4 * reach * zp
    nxt, prv = s + 2 * reach, s - 2 * reach
    sib = f + 1 - 2 * (f % 2)
    far = (f + 2) % 4
    far_sib = (sib + 2) % 4

    def rc(src, dst, ss, rs, seq, fs):
        return pltpu.make_async_remote_copy(
            src_ref=src, dst_ref=dst, send_sem=ss, recv_sem=rs,
            device_id=(seq, fs), device_id_type=MESH,
        )

    barrier = pltpu.get_barrier_semaphore()

    def greet(i, carry):
        pl.semaphore_signal(barrier, inc=1, device_id=((s + i) % seqs, f), device_id_type=MESH)
        return carry

    lax.fori_loop(1, seqs, greet, 0)
    for i in range(1, 4):
        pl.semaphore_signal(barrier, inc=1, device_id=(s, (f + i) % 4), device_id_type=MESH)
    pl.semaphore_wait(barrier, seqs - 1 + 3)

    def held(u, owner, half, c):
        if u < 3:
            n = wrows // 2 // CHUNKS
            at = pl.multiple_of(owner * wrows + half * (wrows // 2) + c * n, 16)
            return wbuf.at[TAPS[u], pl.ds(at, n)]
        n = prows // 2 // CHUNKS
        at = pl.multiple_of(owner * prows + half * (prows // 2) + c * n, 16)
        return pbuf.at[pl.ds(at, n)]

    def mine(u, half, c):
        if u < 3:
            n = wrows // 2 // CHUNKS
            return w_ref.at[TAPS[u], pl.ds(pl.multiple_of(half * (wrows // 2) + c * n, 16), n)]
        n = prows // 2 // CHUNKS
        return p_ref.at[pl.ds(pl.multiple_of(half * (prows // 2) + c * n, 16), n)]

    def held_unit(u, owner):
        if u < 3:
            return wbuf.at[TAPS[u], pl.ds(pl.multiple_of(owner * wrows, 16), wrows)]
        return pbuf.at[pl.ds(pl.multiple_of(owner * prows, 16), prows)]

    def my_unit(u):
        return w_ref.at[TAPS[u]] if u < 3 else p_ref

    def route(j):
        if j >= CHUNKS and j % CHUNKS == CHUNKS - 1:
            return q, mate
        return zp, zmate

    def y_copy(j, owner):
        u, c = j // CHUNKS, j % CHUNKS
        half, unused = route(j)
        return rc(mine(u, half, c), held(u, owner, half, c), y_s.at[j], y_r.at[j], s, far)

    def z_send(j):
        half, partner = route(j)
        piece = held(j // CHUNKS, far, half, j % CHUNKS)
        return rc(piece, piece, z_s.at[j], z_r.at[j], partner, f)

    def z_recv(j):
        half, partner = route(j)
        piece = held(j // CHUNKS, far, 1 - half, j % CHUNKS)
        return rc(piece, piece, z_s.at[j], z_r.at[j], partner, f)

    def a_copy(j, owner):
        piece = held(j // CHUNKS, owner, route(j)[0], j % CHUNKS)
        return rc(piece, piece, a_s.at[j], a_r.at[j], s, sib)

    def b_copy(j, owner):
        piece = held(j // CHUNKS, owner, 1 - route(j)[0], j % CHUNKS)
        return rc(piece, piece, b_s.at[j], b_r.at[j], s, sib)

    def own_copy(u, owner):
        return rc(my_unit(u), held_unit(u, owner), own_s.at[u], own_r.at[u], s, sib)

    def own_local(u):
        return pltpu.make_async_copy(my_unit(u), held_unit(u, f), own_l.at[u])

    def swap(k, slot):
        if k == 0:
            return rc(x_ref.at[1 - q], xbuf.at[slot], sw_s.at[0], sw_r.at[0], mate, f)
        rows = pl.ds((k - 1) * (bins // 2), bins // 2)
        return rc(go_ref.at[1 - q, rows], gbuf.at[slot, rows], sw_s.at[k], sw_r.at[k], mate, f)

    def swap_local(k):
        ref, buf = ((x_ref, xbuf), (go_ref, gbuf))[k]
        return pltpu.make_async_copy(ref.at[q], buf.at[q], sw_l.at[k])

    steps = UNITS * CHUNKS
    swap_local(0).start()
    swap(0, q).start()
    for j in range(AHEAD):
        y_copy(j, f).start()
    for u in range(UNITS):
        own_copy(u, f).start()
        own_local(u).start()
    swap_local(1).start()

    tile = 32
    per = bins // tile

    def first_act(which):
        def go(i, carry):
            at = pl.multiple_of(which * bins + i * tile, tile)
            rows = pl.ds(at, tile)
            v = xbuf[which, pl.ds(pl.multiple_of(i * tile, tile), tile), :].astype(jnp.float32)
            n, scale = normed(v)
            act, slope = gelu_parts(n * g1_ref[...])
            hbuf[rows, :] = act.astype(jnp.bfloat16)
            n1[rows, :] = n
            q1[rows, :] = slope
            r1[rows, :] = jnp.broadcast_to(scale, (tile, 128))
            return carry

        lax.fori_loop(0, per, go, 0)

    def pump(j):
        if j < steps:
            y_copy(j, far).wait_recv()
            z_send(j).start()
            if j + AHEAD < steps:
                y_copy(j + AHEAD, f).start()
            a_copy(j, far).start()
        if j >= LAG:
            z_recv(j - LAG).wait_recv()
            b_copy(j - LAG, far).start()

    def unit_ready(u):
        own_local(u).wait()
        own_copy(u, sib).wait_recv()
        for c in range(CHUNKS):
            a_copy(u * CHUNKS + c, far_sib).wait_recv()
            b_copy(u * CHUNKS + c, far_sib).wait_recv()

    swap_local(0).wait()
    first_act(q)
    pump(0)
    pump(1)
    swap(0, 1 - q).wait_recv()
    first_act(1 - q)
    pump(2)
    pump(3)
    pump(4)
    unit_ready(0)
    swap(1, q).start()

    def fwd(k):
        return dot(hbuf[...], wbuf[k])

    tap = fwd(0)
    acc[bins:, :] = tap[:bins, :]
    psend[0] = tap[bins:, :].astype(jnp.bfloat16)
    last = seqs // (2 * reach) - 1

    def to_next(src, dst, ss, rs):
        return rc(src, dst, ss, rs, nxt, f)

    def to_prev(src, dst, ss, rs):
        return rc(src, dst, ss, rs, prv, f)

    fwd_next = to_next(psend.at[0], rfwd.at[0], fw_s.at[0], fw_r.at[0])
    fwd_prev = to_prev(psend.at[1], rfwd.at[1], fw_s.at[1], fw_r.at[1])
    pl.when(p < last)(lambda: fwd_next.start())
    pump(5)
    pump(6)
    pump(7)
    unit_ready(1)
    swap(2, q).start()
    tap = fwd(2)
    acc[:bins, :] = tap[bins:, :]
    psend[1] = tap[:bins, :].astype(jnp.bfloat16)
    pl.when(p > 0)(lambda: fwd_prev.start())
    pump(8)
    pump(9)
    pump(10)
    pump(11)
    unit_ready(2)
    acc[...] += fwd(1)

    def zero_first():
        rfwd[0] = jnp.zeros_like(rfwd[0])
        gmx[:bins, :] = jnp.zeros((bins, hid), jnp.bfloat16)

    def zero_last():
        rfwd[1] = jnp.zeros_like(rfwd[1])
        gmx[3 * bins:, :] = jnp.zeros((bins, hid), jnp.bfloat16)

    pl.when(p == 0)(zero_first)
    pl.when(p == last)(zero_last)
    pl.when(p > 0)(lambda: fwd_next.wait_recv())
    pl.when(p < last)(lambda: fwd_prev.wait_recv())

    def second_act(i, carry):
        for which in range(2):
            rows = pl.ds(pl.multiple_of(which * bins + i * tile, tile), tile)
            got = rfwd[which, pl.ds(pl.multiple_of(i * tile, tile), tile), :]
            v = (acc[rows, :] + got.astype(jnp.float32)).astype(jnp.bfloat16).astype(jnp.float32)
            n, scale = normed(v)
            unused, slope = gelu_parts(n * g2_ref[...])
            n2[rows, :] = n
            q2[rows, :] = slope
            r2[rows, :] = jnp.broadcast_to(scale, (tile, 128))
        return carry

    lax.fori_loop(0, per, second_act, 0)
    pump(12)
    pump(13)
    swap_local(1).wait()
    swap(1, 1 - q).wait_recv()
    swap(2, 1 - q).wait_recv()
    unit_ready(3)
    acc[...] = dot_t(gbuf[...].reshape(2 * bins, chans), pbuf[...])

    def back(rows, d, n, slope, r, gain, part):
        da = d * slope
        part[...] += fold(da * n)
        dn = da * gain
        m1 = jnp.mean(dn, axis=-1, keepdims=True)
        m2 = jnp.mean(dn * n, axis=-1, keepdims=True)
        return r[rows, 0:1] * (dn - m1 - n * m2)

    part1[...] = jnp.zeros_like(part1)
    part2[...] = jnp.zeros_like(part2)

    def second_back(which):
        def go(i, carry):
            rows = pl.ds(pl.multiple_of(which * bins + i * tile, tile), tile)
            dv = back(rows, acc[rows, :], n2[rows, :], q2[rows, :], r2, g2_ref[...], part2)
            gmx[pl.ds(pl.multiple_of(bins + which * bins + i * tile, tile), tile), :] = dv.astype(jnp.bfloat16)
            return carry

        lax.fori_loop(0, per, go, 0)

    bwd_next = to_next(gmx.at[pl.ds(2 * bins, bins)], gmx.at[pl.ds(0, bins)], bw_s.at[0], bw_r.at[0])
    bwd_prev = to_prev(gmx.at[pl.ds(bins, bins)], gmx.at[pl.ds(3 * bins, bins)], bw_s.at[1], bw_r.at[1])
    second_back(1)
    pl.when(p < last)(lambda: bwd_next.start())
    second_back(0)
    pl.when(p > 0)(lambda: bwd_prev.start())
    gh[...] = dot_t(gmx[bins:3 * bins, :], wbuf[1])
    pl.when(p > 0)(lambda: bwd_next.wait_recv())
    pl.when(p < last)(lambda: bwd_prev.wait_recv())
    gh[...] += dot_t(gmx[2 * bins:, :], wbuf[0])
    gh[...] += dot_t(gmx[:2 * bins, :], wbuf[2])

    def out_mate(i, which):
        rows = pl.ds(pl.multiple_of(i * tile, tile), tile)
        return rc(obuf.at[1 - q, rows], out_ref.at[which, rows], o_s.at[i], o_r.at[i], mate, f)

    def first_back(which, send):
        def go(i, carry):
            rows = pl.ds(pl.multiple_of(which * bins + i * tile, tile), tile)
            here = pl.ds(pl.multiple_of(i * tile, tile), tile)
            dv = back(rows, gh[rows, :], n1[rows, :], q1[rows, :], r1, g1_ref[...], part1)
            obuf[which, here, :] = (gbuf[which, here, :].astype(jnp.float32) + dv).astype(jnp.bfloat16)
            if send:
                out_mate(i, q).start()
            return carry

        lax.fori_loop(0, per, go, 0)

    first_back(1 - q, True)
    first_back(q, False)
    out_own = pltpu.make_async_copy(obuf.at[q], out_ref.at[q], o_l.at[0])
    out_own.start()

    fslots[f, :, :chans] = jnp.sum(part1[...], axis=0, keepdims=True)
    fslots[f, :, chans:] = jnp.sum(part2[...], axis=0, keepdims=True)

    def f_copy(owner, other):
        return rc(fslots.at[owner], fslots.at[owner], gf_s.at[other], gf_r.at[owner], s, other)

    for i in range(1, 4):
        f_copy(f, (f + i) % 4).start()
    for i in range(1, 4):
        f_copy((f + i) % 4, (f + i) % 4).wait_recv()
    sslots[s] = jnp.sum(fslots[...], axis=0)

    def s_copy(owner, other):
        return rc(sslots.at[owner], sslots.at[owner], gs_s.at[other], gs_r.at[owner], other, f)

    def s_send(i, carry):
        s_copy(s, (s + i) % seqs).start()
        return carry

    def s_recv(i, carry):
        s_copy((s + i) % seqs, (s + i) % seqs).wait_recv()
        return carry

    def s_done(i, carry):
        s_copy(s, (s + i) % seqs).wait_send()
        return carry

    lax.fori_loop(1, seqs, s_send, 0)
    lax.fori_loop(1, seqs, s_recv, 0)
    total = jnp.sum(sslots[...], axis=0)
    sum1_ref[...] = total[:, :chans]
    sum2_ref[...] = total[:, chans:]

    lax.fori_loop(1, seqs, s_done, 0)
    for i in range(1, 4):
        f_copy(f, (f + i) % 4).wait_send()
    for j in range(steps):
        y_copy(j, f).wait_send()
        z_send(j).wait_send()
        a_copy(j, far).wait_send()
        b_copy(j, far).wait_send()
    for u in range(UNITS):
        own_copy(u, f).wait_send()
    for k in range(3):
        swap(k, q).wait_send()
    pl.when(p < last)(lambda: fwd_next.wait_send())
    pl.when(p > 0)(lambda: fwd_prev.wait_send())
    pl.when(p < last)(lambda: bwd_next.wait_send())
    pl.when(p > 0)(lambda: bwd_prev.wait_send())
    out_own.wait()
    for i in range(per):
        out_mate(i, q).wait_send()
        out_mate(i, 1 - q).wait_recv()


def body(block_input, dilated_weight, w_project, gain_first, gain_second, grad_output):
    seqs = lax.axis_size("seq")
    fsdps = lax.axis_size("fsdp")
    samples, bins, chans = block_input.shape
    hid = w_project.shape[0] * fsdps
    rows = 2 * bins
    bf16, f32 = jnp.bfloat16, jnp.float32
    dma = lambda n: pltpu.SemaphoreType.DMA((n,))
    steps = UNITS * CHUNKS
    anywhere = pl.BlockSpec(memory_space=pl.ANY)
    vmem = pl.BlockSpec(memory_space=pltpu.VMEM)
    out, sum1, sum2 = pl.pallas_call(
        functools.partial(kernel, seqs),
        out_shape=(
            jax.ShapeDtypeStruct(block_input.shape, bf16),
            jax.ShapeDtypeStruct((1, chans), f32),
            jax.ShapeDtypeStruct((1, hid), f32),
        ),
        in_specs=[anywhere, anywhere, anywhere, vmem, vmem, anywhere],
        out_specs=(anywhere, vmem, vmem),
        scratch_shapes=[
            pltpu.VMEM((2, bins, chans), bf16),
            pltpu.VMEM((2, bins, chans), bf16),
            pltpu.VMEM((3, chans, hid), bf16),
            pltpu.VMEM((hid, chans), bf16),
            pltpu.VMEM((rows, chans), bf16),
            pltpu.VMEM((rows, chans), f32),
            pltpu.VMEM((rows, chans), f32),
            pltpu.VMEM((rows, 128), f32),
            pltpu.VMEM((rows, hid), f32),
            pltpu.VMEM((rows, hid), f32),
            pltpu.VMEM((rows, hid), f32),
            pltpu.VMEM((rows, 128), f32),
            pltpu.VMEM((2, bins, hid), bf16),
            pltpu.VMEM((2, bins, hid), bf16),
            pltpu.VMEM((2 * rows, hid), bf16),
            pltpu.VMEM((rows, chans), f32),
            pltpu.VMEM((2, bins, chans), bf16),
            pltpu.VMEM((8, chans), f32),
            pltpu.VMEM((8, hid), f32),
            pltpu.VMEM((fsdps, 1, chans + hid), f32),
            pltpu.VMEM((seqs, 1, chans + hid), f32),
        ]
        + [dma(steps)] * 8
        + [dma(UNITS)] * 3
        + [dma(3)] * 2
        + [dma(2)] * 5
        + [dma(bins // 32)] * 2
        + [dma(1)]
        + [dma(fsdps)] * 2
        + [dma(seqs)] * 2,
        compiler_params=pltpu.CompilerParams(
            collective_id=0, has_side_effects=True, vmem_limit_bytes=62 * 1024 * 1024
        ),
    )(
        block_input, dilated_weight, w_project,
        gain_first.reshape(1, chans), gain_second.reshape(1, hid), grad_output,
    )
    return out, sum1.reshape(chans), sum2.reshape(hid)


def solution(mesh):
    in_specs = (
        P("fsdp", "seq", None),
        P(None, "fsdp", None),
        P("fsdp", None),
        P(),
        P(),
        P("fsdp", "seq", None),
    )
    out_specs = (P("fsdp", "seq", None), P(), P())
    return jax.shard_map(body, mesh=mesh, in_specs=in_specs, out_specs=out_specs, check_vma=False)
```

```python
import functools

import jax
import jax.numpy as jnp
from jax import lax
from jax.experimental import pallas as pl
from jax.experimental.pallas import tpu as pltpu
from jax.sharding import PartitionSpec as P

MESH = pl.DeviceIdType.MESH
TAPS = (0, 2, 1)
CHUNKS = 3
LAG = 2
AHEAD = 3
UNITS = 4
EPS = 1e-05
K0 = 0.7978845608028654
K1 = 0.044715


def normed(values):
    centre = values - jnp.mean(values, axis=-1, keepdims=True)
    scale = lax.rsqrt(jnp.mean(centre * centre, axis=-1, keepdims=True) + EPS)
    return centre * scale, scale


def gelu_parts(a):
    square = a * a
    t = jnp.tanh(a * (K0 + (K0 * K1) * square))
    half = 0.5 + 0.5 * t
    slope = half + (0.5 * a) * (1.0 - t * t) * (K0 + (3.0 * K0 * K1) * square)
    return a * half, slope


def dot(a, b):
    return jnp.dot(a, b, preferred_element_type=jnp.float32)


def dot_t(a, b):
    return lax.dot_general(a, b, (((1,), (1,)), ((), ())), preferred_element_type=jnp.float32)


def fold(values):
    rows, columns = values.shape
    return jnp.sum(values.reshape(rows // 8, 8, columns), axis=0)


def kernel(
    seqs, x_ref, w_ref, p_ref, g1_ref, g2_ref, go_ref,
    out_ref, sum1_ref, sum2_ref,
    xbuf, gbuf, wbuf, pbuf, hbuf, n1, q1, r1, acc, n2, q2, r2, psend, rfwd, gmx, gh, ght, g2t, obuf,
    part1, part2, fslots, sslots,
    y_s, y_r, z_s, z_r, a_s, a_r, b_s, b_r, own_s, own_r, own_l,
    sw_s, sw_r, sw_l, fw_s, fw_r, bw_s, bw_r, o_s, o_r, o_l, gf_s, gf_r, gs_s, gs_r,
):
    bins, chans = xbuf.shape[1], xbuf.shape[2]
    hid = pbuf.shape[0]
    wrows, prows = w_ref.shape[1], p_ref.shape[0]
    s, f = lax.axis_index("seq"), lax.axis_index("fsdp")
    reach = seqs // 8
    block = s // reach
    p, q = block // 2, block % 2
    zp = p % 2
    mate = s + reach - 2 * reach * q
    zmate = s + 2 * reach - 4 * reach * zp
    nxt, prv = s + 2 * reach, s - 2 * reach
    sib = f + 1 - 2 * (f % 2)
    far = (f + 2) % 4
    far_sib = (sib + 2) % 4

    def rc(src, dst, ss, rs, seq, fs):
        return pltpu.make_async_remote_copy(
            src_ref=src, dst_ref=dst, send_sem=ss, recv_sem=rs,
            device_id=(seq, fs), device_id_type=MESH,
        )

    barrier = pltpu.get_barrier_semaphore()

    def greet(i, carry):
        pl.semaphore_signal(barrier, inc=1, device_id=((s + i) % seqs, f), device_id_type=MESH)
        return carry

    lax.fori_loop(1, seqs, greet, 0)
    for i in range(1, 4):
        pl.semaphore_signal(barrier, inc=1, device_id=(s, (f + i) % 4), device_id_type=MESH)
    pl.semaphore_wait(barrier, seqs - 1 + 3)

    def held(u, owner, half, c):
        if u < 3:
            n = wrows // 2 // CHUNKS
            at = pl.multiple_of(owner * wrows + half * (wrows // 2) + c * n, 16)
            return wbuf.at[TAPS[u], pl.ds(at, n)]
        n = prows // 2 // CHUNKS
        at = pl.multiple_of(owner * prows + half * (prows // 2) + c * n, 16)
        return pbuf.at[pl.ds(at, n)]

    def mine(u, half, c):
        if u < 3:
            n = wrows // 2 // CHUNKS
            return w_ref.at[TAPS[u], pl.ds(pl.multiple_of(half * (wrows // 2) + c * n, 16), n)]
        n = prows // 2 // CHUNKS
        return p_ref.at[pl.ds(pl.multiple_of(half * (prows // 2) + c * n, 16), n)]

    def held_unit(u, owner):
        if u < 3:
            return wbuf.at[TAPS[u], pl.ds(pl.multiple_of(owner * wrows, 16), wrows)]
        return pbuf.at[pl.ds(pl.multiple_of(owner * prows, 16), prows)]

    def my_unit(u):
        return w_ref.at[TAPS[u]] if u < 3 else p_ref

    def route(j):
        if j >= CHUNKS and j % CHUNKS == CHUNKS - 1:
            return q, mate
        return zp, zmate

    def y_copy(j, owner):
        u, c = j // CHUNKS, j % CHUNKS
        half, unused = route(j)
        return rc(mine(u, half, c), held(u, owner, half, c), y_s.at[j], y_r.at[j], s, far)

    def z_send(j):
        half, partner = route(j)
        piece = held(j // CHUNKS, far, half, j % CHUNKS)
        return rc(piece, piece, z_s.at[j], z_r.at[j], partner, f)

    def z_recv(j):
        half, partner = route(j)
        piece = held(j // CHUNKS, far, 1 - half, j % CHUNKS)
        return rc(piece, piece, z_s.at[j], z_r.at[j], partner, f)

    def a_copy(j, owner):
        piece = held(j // CHUNKS, owner, route(j)[0], j % CHUNKS)
        return rc(piece, piece, a_s.at[j], a_r.at[j], s, sib)

    def b_copy(j, owner):
        piece = held(j // CHUNKS, owner, 1 - route(j)[0], j % CHUNKS)
        return rc(piece, piece, b_s.at[j], b_r.at[j], s, sib)

    def own_copy(u, owner):
        return rc(my_unit(u), held_unit(u, owner), own_s.at[u], own_r.at[u], s, sib)

    def own_local(u):
        return pltpu.make_async_copy(my_unit(u), held_unit(u, f), own_l.at[u])

    def swap(k, slot):
        if k == 0:
            return rc(x_ref.at[1 - q], xbuf.at[slot], sw_s.at[0], sw_r.at[0], mate, f)
        rows = pl.ds((k - 1) * (bins // 2), bins // 2)
        return rc(go_ref.at[1 - q, rows], gbuf.at[slot, rows], sw_s.at[k], sw_r.at[k], mate, f)

    def swap_local(k):
        ref, buf = ((x_ref, xbuf), (go_ref, gbuf))[k]
        return pltpu.make_async_copy(ref.at[q], buf.at[q], sw_l.at[k])

    steps = UNITS * CHUNKS
    swap_local(0).start()
    swap(0, q).start()
    for j in range(AHEAD):
        y_copy(j, f).start()
    for u in range(UNITS):
        own_copy(u, f).start()
        own_local(u).start()
    swap_local(1).start()

    tile = 32
    per = bins // tile

    def first_act(which):
        def go(i, carry):
            at = pl.multiple_of(which * bins + i * tile, tile)
            rows = pl.ds(at, tile)
            v = xbuf[which, pl.ds(pl.multiple_of(i * tile, tile), tile), :].astype(jnp.float32)
            n, scale = normed(v)
            act, slope = gelu_parts(n * g1_ref[...])
            hbuf[rows, :] = act.astype(jnp.bfloat16)
            n1[rows, :] = n
            q1[rows, :] = slope
            r1[rows, :] = jnp.broadcast_to(scale, (tile, 128))
            return carry

        lax.fori_loop(0, per, go, 0)

    def pump(j):
        if j < steps:
            y_copy(j, far).wait_recv()
            z_send(j).start()
            if j + AHEAD < steps:
                y_copy(j + AHEAD, f).start()
            a_copy(j, far).start()
        if j >= LAG:
            z_recv(j - LAG).wait_recv()
            b_copy(j - LAG, far).start()

    def near_ready(u):
        own_local(u).wait()
        own_copy(u, sib).wait_recv()

    def unit_ready(u):
        for c in range(CHUNKS):
            a_copy(u * CHUNKS + c, far_sib).wait_recv()
            b_copy(u * CHUNKS + c, far_sib).wait_recv()

    side = f // 2

    def span(which, size):
        return pl.ds(pl.multiple_of(which * size, 128), size)

    def fwd(k, which):
        rows = span(which, 2 * wrows)
        return dot(hbuf[:, rows], wbuf[k, rows, :])

    swap_local(0).wait()
    first_act(q)
    pump(0)
    pump(1)
    swap(0, 1 - q).wait_recv()
    first_act(1 - q)
    pump(2)
    near_ready(0)
    n2[...] = fwd(0, side)
    pump(3)
    near_ready(1)
    q2[...] = fwd(2, side)
    pump(4)
    near_ready(2)
    acc[...] = fwd(1, side)
    unit_ready(0)
    swap(1, q).start()

    n2[...] += fwd(0, 1 - side)
    acc[bins:, :] += n2[:bins, :]
    psend[0] = n2[bins:, :].astype(jnp.bfloat16)
    last = seqs // (2 * reach) - 1

    def to_next(src, dst, ss, rs):
        return rc(src, dst, ss, rs, nxt, f)

    def to_prev(src, dst, ss, rs):
        return rc(src, dst, ss, rs, prv, f)

    fwd_next = to_next(psend.at[0], rfwd.at[0], fw_s.at[0], fw_r.at[0])
    fwd_prev = to_prev(psend.at[1], rfwd.at[1], fw_s.at[1], fw_r.at[1])
    pl.when(p < last)(lambda: fwd_next.start())
    pump(5)
    pump(6)
    pump(7)
    unit_ready(1)
    swap(2, q).start()
    q2[...] += fwd(2, 1 - side)
    acc[:bins, :] += q2[bins:, :]
    psend[1] = q2[:bins, :].astype(jnp.bfloat16)
    pl.when(p > 0)(lambda: fwd_prev.start())
    pump(8)
    pump(9)
    pump(10)
    pump(11)
    unit_ready(2)
    acc[...] += fwd(1, 1 - side)

    def zero_first():
        rfwd[0] = jnp.zeros_like(rfwd[0])
        gmx[:bins, :] = jnp.zeros((bins, hid), jnp.bfloat16)

    def zero_last():
        rfwd[1] = jnp.zeros_like(rfwd[1])
        gmx[3 * bins:, :] = jnp.zeros((bins, hid), jnp.bfloat16)

    pl.when(p == 0)(zero_first)
    pl.when(p == last)(zero_last)
    pl.when(p > 0)(lambda: fwd_next.wait_recv())
    pl.when(p < last)(lambda: fwd_prev.wait_recv())

    def second_act(i, carry):
        for which in range(2):
            rows = pl.ds(pl.multiple_of(which * bins + i * tile, tile), tile)
            got = rfwd[which, pl.ds(pl.multiple_of(i * tile, tile), tile), :]
            v = (acc[rows, :] + got.astype(jnp.float32)).astype(jnp.bfloat16).astype(jnp.float32)
            n, scale = normed(v)
            unused, slope = gelu_parts(n * g2_ref[...])
            n2[rows, :] = n
            q2[rows, :] = slope
            r2[rows, :] = jnp.broadcast_to(scale, (tile, 128))
        return carry

    lax.fori_loop(0, per, second_act, 0)
    pump(12)
    swap_local(1).wait()
    swap(1, 1 - q).wait_recv()
    swap(2, 1 - q).wait_recv()
    near_ready(3)

    def grad_hidden2(which):
        rows = span(which, 2 * prows)
        g2t[rows, :] = dot_t(pbuf[rows, :], gbuf[...].reshape(2 * bins, chans))

    grad_hidden2(side)
    pump(13)
    unit_ready(3)
    grad_hidden2(1 - side)

    def back(rows, d, n, slope, r, gain, part):
        da = d * slope
        part[...] += fold(da * n)
        dn = da * gain
        m1 = jnp.mean(dn, axis=-1, keepdims=True)
        m2 = jnp.mean(dn * n, axis=-1, keepdims=True)
        return r[rows, 0:1] * (dn - m1 - n * m2)

    part1[...] = jnp.zeros_like(part1)
    part2[...] = jnp.zeros_like(part2)

    def second_back(which):
        def go(i, carry):
            rows = pl.ds(pl.multiple_of(which * bins + i * tile, tile), tile)
            dv = back(rows, acc[rows, :], n2[rows, :], q2[rows, :], r2, g2_ref[...], part2)
            gmx[pl.ds(pl.multiple_of(bins + which * bins + i * tile, tile), tile), :] = dv.astype(jnp.bfloat16)
            return carry

        acc[which * bins:(which + 1) * bins, :] = g2t[:, which * bins:(which + 1) * bins].T
        lax.fori_loop(0, per, go, 0)

    bwd_next = to_next(gmx.at[pl.ds(2 * bins, bins)], gmx.at[pl.ds(0, bins)], bw_s.at[0], bw_r.at[0])
    bwd_prev = to_prev(gmx.at[pl.ds(bins, bins)], gmx.at[pl.ds(3 * bins, bins)], bw_s.at[1], bw_r.at[1])
    second_back(1)
    pl.when(p < last)(lambda: bwd_next.start())
    second_back(0)
    pl.when(p > 0)(lambda: bwd_prev.start())
    ght[...] = dot_t(wbuf[1], gmx[bins:3 * bins, :])
    pl.when(p > 0)(lambda: bwd_next.wait_recv())
    pl.when(p < last)(lambda: bwd_prev.wait_recv())
    ght[...] += dot_t(wbuf[0], gmx[2 * bins:, :])
    ght[...] += dot_t(wbuf[2], gmx[:2 * bins, :])
    for i in range(2):
        gh[i * bins:(i + 1) * bins, :] = ght[:, i * bins:(i + 1) * bins].T

    def out_mate(i, which):
        rows = pl.ds(pl.multiple_of(i * tile, tile), tile)
        return rc(obuf.at[1 - q, rows], out_ref.at[which, rows], o_s.at[i], o_r.at[i], mate, f)

    def first_back(which, send):
        def go(i, carry):
            rows = pl.ds(pl.multiple_of(which * bins + i * tile, tile), tile)
            here = pl.ds(pl.multiple_of(i * tile, tile), tile)
            dv = back(rows, gh[rows, :], n1[rows, :], q1[rows, :], r1, g1_ref[...], part1)
            obuf[which, here, :] = (gbuf[which, here, :].astype(jnp.float32) + dv).astype(jnp.bfloat16)
            if send:
                out_mate(i, q).start()
            return carry

        lax.fori_loop(0, per, go, 0)

    first_back(1 - q, True)
    first_back(q, False)
    out_own = pltpu.make_async_copy(obuf.at[q], out_ref.at[q], o_l.at[0])
    out_own.start()

    fslots[f, :, :chans] = jnp.sum(part1[...], axis=0, keepdims=True)
    fslots[f, :, chans:] = jnp.sum(part2[...], axis=0, keepdims=True)

    def f_copy(owner, other):
        return rc(fslots.at[owner], fslots.at[owner], gf_s.at[other], gf_r.at[owner], s, other)

    for i in range(1, 4):
        f_copy(f, (f + i) % 4).start()
    for i in range(1, 4):
        f_copy((f + i) % 4, (f + i) % 4).wait_recv()
    sslots[s] = jnp.sum(fslots[...], axis=0)

    def s_copy(owner, other):
        return rc(sslots.at[owner], sslots.at[owner], gs_s.at[other], gs_r.at[owner], other, f)

    def s_send(i, carry):
        s_copy(s, (s + i) % seqs).start()
        return carry

    def s_recv(i, carry):
        s_copy((s + i) % seqs, (s + i) % seqs).wait_recv()
        return carry

    def s_done(i, carry):
        s_copy(s, (s + i) % seqs).wait_send()
        return carry

    lax.fori_loop(1, seqs, s_send, 0)
    lax.fori_loop(1, seqs, s_recv, 0)
    total = jnp.sum(sslots[...], axis=0)
    sum1_ref[...] = total[:, :chans]
    sum2_ref[...] = total[:, chans:]

    lax.fori_loop(1, seqs, s_done, 0)
    for i in range(1, 4):
        f_copy(f, (f + i) % 4).wait_send()
    for j in range(steps):
        y_copy(j, f).wait_send()
        z_send(j).wait_send()
        a_copy(j, far).wait_send()
        b_copy(j, far).wait_send()
    for u in range(UNITS):
        own_copy(u, f).wait_send()
    for k in range(3):
        swap(k, q).wait_send()
    pl.when(p < last)(lambda: fwd_next.wait_send())
    pl.when(p > 0)(lambda: fwd_prev.wait_send())
    pl.when(p < last)(lambda: bwd_next.wait_send())
    pl.when(p > 0)(lambda: bwd_prev.wait_send())
    out_own.wait()
    for i in range(per):
        out_mate(i, q).wait_send()
        out_mate(i, 1 - q).wait_recv()


def body(block_input, dilated_weight, w_project, gain_first, gain_second, grad_output):
    seqs = lax.axis_size("seq")
    fsdps = lax.axis_size("fsdp")
    samples, bins, chans = block_input.shape
    hid = w_project.shape[0] * fsdps
    rows = 2 * bins
    bf16, f32 = jnp.bfloat16, jnp.float32
    dma = lambda n: pltpu.SemaphoreType.DMA((n,))
    steps = UNITS * CHUNKS
    anywhere = pl.BlockSpec(memory_space=pl.ANY)
    hbm = pl.BlockSpec(memory_space=pltpu.HBM)
    vmem = pl.BlockSpec(memory_space=pltpu.VMEM)
    out, sum1, sum2 = pl.pallas_call(
        functools.partial(kernel, seqs),
        out_shape=(
            jax.ShapeDtypeStruct(block_input.shape, bf16),
            jax.ShapeDtypeStruct((1, chans), f32),
            jax.ShapeDtypeStruct((1, hid), f32),
        ),
        in_specs=[hbm, hbm, hbm, vmem, vmem, hbm],
        out_specs=(anywhere, vmem, vmem),
        scratch_shapes=[
            pltpu.VMEM((2, bins, chans), bf16),
            pltpu.VMEM((2, bins, chans), bf16),
            pltpu.VMEM((3, chans, hid), bf16),
            pltpu.VMEM((hid, chans), bf16),
            pltpu.VMEM((rows, chans), bf16),
            pltpu.VMEM((rows, chans), f32),
            pltpu.VMEM((rows, chans), f32),
            pltpu.VMEM((rows, 128), f32),
            pltpu.VMEM((rows, hid), f32),
            pltpu.VMEM((rows, hid), f32),
            pltpu.VMEM((rows, hid), f32),
            pltpu.VMEM((rows, 128), f32),
            pltpu.VMEM((2, bins, hid), bf16),
            pltpu.VMEM((2, bins, hid), bf16),
            pltpu.VMEM((2 * rows, hid), bf16),
            pltpu.VMEM((rows, chans), f32),
            pltpu.VMEM((chans, rows), f32),
            pltpu.VMEM((hid, rows), f32),
            pltpu.VMEM((2, bins, chans), bf16),
            pltpu.VMEM((8, chans), f32),
            pltpu.VMEM((8, hid), f32),
            pltpu.VMEM((fsdps, 1, chans + hid), f32),
            pltpu.VMEM((seqs, 1, chans + hid), f32),
        ]
        + [dma(steps)] * 8
        + [dma(UNITS)] * 3
        + [dma(3)] * 2
        + [dma(2)] * 5
        + [dma(bins // 32)] * 2
        + [dma(1)]
        + [dma(fsdps)] * 2
        + [dma(seqs)] * 2,
        compiler_params=pltpu.CompilerParams(
            collective_id=0, has_side_effects=True, vmem_limit_bytes=52 * 1024 * 1024
        ),
    )(
        block_input, dilated_weight, w_project,
        gain_first.reshape(1, chans), gain_second.reshape(1, hid), grad_output,
    )
    return out, sum1.reshape(chans), sum2.reshape(hid)


def solution(mesh):
    in_specs = (
        P("fsdp", "seq", None),
        P(None, "fsdp", None),
        P("fsdp", None),
        P(),
        P(),
        P("fsdp", "seq", None),
    )
    out_specs = (P("fsdp", "seq", None), P(), P())
    return jax.shard_map(body, mesh=mesh, in_specs=in_specs, out_specs=out_specs, check_vma=False)
```

```python
import functools

import jax
import jax.numpy as jnp
from jax import lax
from jax.experimental import pallas as pl
from jax.experimental.pallas import tpu as pltpu
from jax.sharding import PartitionSpec as P

MESH = pl.DeviceIdType.MESH
TAPS = (0, 2, 1)
GROUPS = 2
CHUNKS = 3
LAG = 2
AHEAD = 5
UNITS = 4
EPS = 1e-05
K0 = 0.7978845608028654
K1 = 0.044715


def normed(values):
    centre = values - jnp.mean(values, axis=-1, keepdims=True)
    scale = lax.rsqrt(jnp.mean(centre * centre, axis=-1, keepdims=True) + EPS)
    return centre * scale, scale


def gelu_parts(a):
    square = a * a
    t = jnp.tanh(a * (K0 + (K0 * K1) * square))
    half = 0.5 + 0.5 * t
    slope = half + (0.5 * a) * (1.0 - t * t) * (K0 + (3.0 * K0 * K1) * square)
    return a * half, slope


def dot(a, b):
    return jnp.dot(a, b, preferred_element_type=jnp.float32)


def dot_t(a, b):
    return lax.dot_general(a, b, (((1,), (1,)), ((), ())), preferred_element_type=jnp.float32)


def fold(values):
    rows, columns = values.shape
    return jnp.sum(values.reshape(rows // 8, 8, columns), axis=0)


def kernel(
    seqs, x_ref, w_ref, p_ref, g1_ref, g2_ref, go_ref,
    out_ref, sum1_ref, sum2_ref,
    xbuf, gbuf, wbuf, pbuf, hbuf, n1, q1, r1, acc, n2, q2, r2, psend, rfwd, gmx, gh, ght, g2t, obuf,
    part1, part2, fslots, sslots,
    y_s, y_r, z_s, z_r, a_s, a_r, b_s, b_r, own_s, own_r, own_l,
    sw_s, sw_r, sw_l, fw_s, fw_r, bw_s, bw_r, o_s, o_r, o_l, gf_s, gf_r, gs_s, gs_r,
):
    bins, chans = xbuf.shape[1], xbuf.shape[2]
    hid = pbuf.shape[0]
    wrows, prows = w_ref.shape[1], p_ref.shape[0]
    s, f = lax.axis_index("seq"), lax.axis_index("fsdp")
    reach = seqs // 8
    block = s // reach
    p, q = block // 2, block % 2
    zp = p % 2
    mate = s + reach - 2 * reach * q
    zmate = s + 2 * reach - 4 * reach * zp
    nxt, prv = s + 2 * reach, s - 2 * reach
    sib = f + 1 - 2 * (f % 2)
    far = (f + 2) % 4
    far_sib = (sib + 2) % 4

    def rc(src, dst, ss, rs, seq, fs):
        return pltpu.make_async_remote_copy(
            src_ref=src, dst_ref=dst, send_sem=ss, recv_sem=rs,
            device_id=(seq, fs), device_id_type=MESH,
        )

    barrier = pltpu.get_barrier_semaphore()

    def greet(i, carry):
        pl.semaphore_signal(barrier, inc=1, device_id=((s + i) % seqs, f), device_id_type=MESH)
        return carry

    lax.fori_loop(1, seqs, greet, 0)
    for i in range(1, 4):
        pl.semaphore_signal(barrier, inc=1, device_id=(s, (f + i) % 4), device_id_type=MESH)
    pl.semaphore_wait(barrier, seqs - 1 + 3)

    def held(u, owner, half, c):
        if u < 3:
            n = wrows // 2 // CHUNKS
            at = pl.multiple_of(owner * wrows + half * (wrows // 2) + c * n, 16)
            return wbuf.at[TAPS[u], pl.ds(at, n)]
        n = prows // 2 // CHUNKS
        at = pl.multiple_of(owner * prows + half * (prows // 2) + c * n, 16)
        return pbuf.at[pl.ds(at, n)]

    def mine(u, half, c):
        if u < 3:
            n = wrows // 2 // CHUNKS
            return w_ref.at[TAPS[u], pl.ds(pl.multiple_of(half * (wrows // 2) + c * n, 16), n)]
        n = prows // 2 // CHUNKS
        return p_ref.at[pl.ds(pl.multiple_of(half * (prows // 2) + c * n, 16), n)]

    def held_unit(u, owner):
        if u < 3:
            return wbuf.at[TAPS[u], pl.ds(pl.multiple_of(owner * wrows, 16), wrows)]
        return pbuf.at[pl.ds(pl.multiple_of(owner * prows, 16), prows)]

    def my_unit(u):
        return w_ref.at[TAPS[u]] if u < 3 else p_ref

    def route(j):
        if j >= CHUNKS and j % CHUNKS == CHUNKS - 1:
            return q, mate
        return zp, zmate

    def y_copy(j, owner):
        u, c = j // CHUNKS, j % CHUNKS
        half, unused = route(j)
        return rc(mine(u, half, c), held(u, owner, half, c), y_s.at[j], y_r.at[j], s, far)

    def z_send(j):
        half, partner = route(j)
        piece = held(j // CHUNKS, far, half, j % CHUNKS)
        return rc(piece, piece, z_s.at[j], z_r.at[j], partner, f)

    def z_recv(j):
        half, partner = route(j)
        piece = held(j // CHUNKS, far, 1 - half, j % CHUNKS)
        return rc(piece, piece, z_s.at[j], z_r.at[j], partner, f)

    def a_copy(j, owner):
        piece = held(j // CHUNKS, owner, route(j)[0], j % CHUNKS)
        return rc(piece, piece, a_s.at[j], a_r.at[j], s, sib)

    def b_copy(j, owner):
        piece = held(j // CHUNKS, owner, 1 - route(j)[0], j % CHUNKS)
        return rc(piece, piece, b_s.at[j], b_r.at[j], s, sib)

    def own_copy(u, owner):
        return rc(my_unit(u), held_unit(u, owner), own_s.at[u], own_r.at[u], s, sib)

    def own_local(u):
        return pltpu.make_async_copy(my_unit(u), held_unit(u, f), own_l.at[u])

    def swap(k, slot):
        if k == 0:
            return rc(x_ref.at[1 - q], xbuf.at[slot], sw_s.at[0], sw_r.at[0], mate, f)
        rows = pl.ds((k - 1) * (bins // 2), bins // 2)
        return rc(go_ref.at[1 - q, rows], gbuf.at[slot, rows], sw_s.at[k], sw_r.at[k], mate, f)

    def swap_local(k):
        ref, buf = ((x_ref, xbuf), (go_ref, gbuf))[k]
        return pltpu.make_async_copy(ref.at[q], buf.at[q], sw_l.at[k])

    steps = UNITS * CHUNKS
    swap_local(0).start()
    swap(0, q).start()
    for j in range(AHEAD):
        y_copy(j, f).start()
    for u in range(UNITS):
        own_copy(u, f).start()
        own_local(u).start()
    swap_local(1).start()

    tile = 32
    per = bins // tile

    def first_act(which):
        def go(i, carry):
            at = pl.multiple_of(which * bins + i * tile, tile)
            rows = pl.ds(at, tile)
            v = xbuf[which, pl.ds(pl.multiple_of(i * tile, tile), tile), :].astype(jnp.float32)
            n, scale = normed(v)
            act, slope = gelu_parts(n * g1_ref[...])
            hbuf[rows, :] = act.astype(jnp.bfloat16)
            n1[rows, :] = n
            q1[rows, :] = slope
            r1[rows, :] = jnp.broadcast_to(scale, (tile, 128))
            return carry

        lax.fori_loop(0, per, go, 0)

    def pump(j):
        if j < steps:
            y_copy(j, far).wait_recv()
            z_send(j).start()
            if j + AHEAD < steps:
                y_copy(j + AHEAD, f).start()
            a_copy(j, far).start()
        if j >= LAG:
            z_recv(j - LAG).wait_recv()
            b_copy(j - LAG, far).start()

    def near_ready(u):
        own_local(u).wait()
        own_copy(u, sib).wait_recv()

    def unit_ready(u):
        for c in range(CHUNKS):
            a_copy(u * CHUNKS + c, far_sib).wait_recv()
            b_copy(u * CHUNKS + c, far_sib).wait_recv()

    side = f // 2

    def span(which, size):
        return pl.ds(pl.multiple_of(which * size, 128), size)

    def fwd(k, which):
        rows = span(which, 2 * wrows)
        return dot(hbuf[:, rows], wbuf[k, rows, :])

    swap_local(0).wait()
    first_act(q)
    pump(0)
    pump(1)
    swap(0, 1 - q).wait_recv()
    first_act(1 - q)
    pump(2)
    near_ready(0)
    n2[...] = fwd(0, side)
    pump(3)
    near_ready(1)
    q2[...] = fwd(2, side)
    pump(4)
    near_ready(2)
    acc[...] = fwd(1, side)
    unit_ready(0)
    swap(1, q).start()

    n2[...] += fwd(0, 1 - side)
    acc[bins:, :] += n2[:bins, :]
    psend[0] = n2[bins:, :].astype(jnp.bfloat16)
    last = seqs // (2 * reach) - 1

    def to_next(src, dst, ss, rs):
        return rc(src, dst, ss, rs, nxt, f)

    def to_prev(src, dst, ss, rs):
        return rc(src, dst, ss, rs, prv, f)

    fwd_next = to_next(psend.at[0], rfwd.at[0], fw_s.at[0], fw_r.at[0])
    fwd_prev = to_prev(psend.at[1], rfwd.at[1], fw_s.at[1], fw_r.at[1])
    pl.when(p < last)(lambda: fwd_next.start())
    pump(5)
    pump(6)
    pump(7)
    unit_ready(1)
    swap(2, q).start()
    q2[...] += fwd(2, 1 - side)
    acc[:bins, :] += q2[bins:, :]
    psend[1] = q2[:bins, :].astype(jnp.bfloat16)
    pl.when(p > 0)(lambda: fwd_prev.start())
    pump(8)
    pump(9)
    pump(10)
    pump(11)
    unit_ready(2)
    acc[...] += fwd(1, 1 - side)

    part = bins // GROUPS

    def zero_first():
        rfwd[0] = jnp.zeros_like(rfwd[0])
        gmx[:, :part, :] = jnp.zeros((GROUPS, part, hid), jnp.bfloat16)

    def zero_last():
        rfwd[1] = jnp.zeros_like(rfwd[1])
        gmx[:, 3 * part:, :] = jnp.zeros((GROUPS, part, hid), jnp.bfloat16)

    pl.when(p == 0)(zero_first)
    pl.when(p == last)(zero_last)
    pl.when(p > 0)(lambda: fwd_next.wait_recv())
    pl.when(p < last)(lambda: fwd_prev.wait_recv())

    def second_act(i, carry):
        for which in range(2):
            rows = pl.ds(pl.multiple_of(which * bins + i * tile, tile), tile)
            got = rfwd[which, pl.ds(pl.multiple_of(i * tile, tile), tile), :]
            v = (acc[rows, :] + got.astype(jnp.float32)).astype(jnp.bfloat16).astype(jnp.float32)
            n, scale = normed(v)
            unused, slope = gelu_parts(n * g2_ref[...])
            n2[rows, :] = n
            q2[rows, :] = slope
            r2[rows, :] = jnp.broadcast_to(scale, (tile, 128))
        return carry

    lax.fori_loop(0, per, second_act, 0)
    pump(12)
    swap_local(1).wait()
    swap(1, 1 - q).wait_recv()
    swap(2, 1 - q).wait_recv()
    near_ready(3)

    def grad_hidden2(which):
        rows = span(which, 2 * prows)
        g2t[rows, :] = dot_t(pbuf[rows, :], gbuf[...].reshape(2 * bins, chans))

    grad_hidden2(side)
    pump(13)
    unit_ready(3)
    grad_hidden2(1 - side)

    def back(rows, d, n, slope, r, gain, total):
        da = d * slope
        total[...] += fold(da * n)
        dn = da * gain
        m1 = jnp.mean(dn, axis=-1, keepdims=True)
        m2 = jnp.mean(dn * n, axis=-1, keepdims=True)
        return r[rows, 0:1] * (dn - m1 - n * m2)

    part1[...] = jnp.zeros_like(part1)
    part2[...] = jnp.zeros_like(part2)

    for i in range(2):
        acc[i * bins:(i + 1) * bins, :] = g2t[:, i * bins:(i + 1) * bins].T
    each = part // tile

    def second_back(g, which):
        def go(i, carry):
            at = g * part + i * tile
            rows = pl.ds(pl.multiple_of(which * bins + at, tile), tile)
            dv = back(rows, acc[rows, :], n2[rows, :], q2[rows, :], r2, g2_ref[...], part2)
            to = pl.ds(pl.multiple_of((1 + which) * part + i * tile, tile), tile)
            gmx[g, to, :] = dv.astype(jnp.bfloat16)
            return carry

        lax.fori_loop(0, each, go, 0)

    def bwd_next(g):
        src, dst = gmx.at[g, pl.ds(2 * part, part)], gmx.at[g, pl.ds(0, part)]
        return to_next(src, dst, bw_s.at[2 * g], bw_r.at[2 * g])

    def bwd_prev(g):
        src, dst = gmx.at[g, pl.ds(part, part)], gmx.at[g, pl.ds(3 * part, part)]
        return to_prev(src, dst, bw_s.at[2 * g + 1], bw_r.at[2 * g + 1])

    for g in range(GROUPS):
        second_back(g, 1)
        pl.when(p < last)(lambda: bwd_next(g).start())
        second_back(g, 0)
        pl.when(p > 0)(lambda: bwd_prev(g).start())

    def out_mate(i, which):
        rows = pl.ds(pl.multiple_of(i * tile, tile), tile)
        return rc(obuf.at[1 - q, rows], out_ref.at[which, rows], o_s.at[i], o_r.at[i], mate, f)

    def first_back(g, which, send):
        def go(i, carry):
            rows = pl.ds(pl.multiple_of(which * part + i * tile, tile), tile)
            at = g * part + i * tile
            all_rows = pl.ds(pl.multiple_of(which * bins + at, tile), tile)
            here = pl.ds(pl.multiple_of(at, tile), tile)
            dv = back(all_rows, gh[rows, :], n1[all_rows, :], q1[all_rows, :], r1, g1_ref[...], part1)
            obuf[which, here, :] = (gbuf[which, here, :].astype(jnp.float32) + dv).astype(jnp.bfloat16)
            if send:
                out_mate(g * each + i, q).start()
            return carry

        lax.fori_loop(0, each, go, 0)

    for g in range(GROUPS):
        ght[...] = dot_t(wbuf[1], gmx[g, part:3 * part, :])
        pl.when(p > 0)(lambda: bwd_next(g).wait_recv())
        pl.when(p < last)(lambda: bwd_prev(g).wait_recv())
        ght[...] += dot_t(wbuf[0], gmx[g, 2 * part:, :])
        ght[...] += dot_t(wbuf[2], gmx[g, :2 * part, :])
        gh[...] = ght[...].T
        first_back(g, 1 - q, True)
        first_back(g, q, False)
    out_own = pltpu.make_async_copy(obuf.at[q], out_ref.at[q], o_l.at[0])
    out_own.start()

    fslots[f, :, :chans] = jnp.sum(part1[...], axis=0, keepdims=True)
    fslots[f, :, chans:] = jnp.sum(part2[...], axis=0, keepdims=True)

    def f_copy(owner, other):
        return rc(fslots.at[owner], fslots.at[owner], gf_s.at[other], gf_r.at[owner], s, other)

    for i in range(1, 4):
        f_copy(f, (f + i) % 4).start()
    for i in range(1, 4):
        f_copy((f + i) % 4, (f + i) % 4).wait_recv()
    sslots[s] = jnp.sum(fslots[...], axis=0)

    def s_copy(owner, other):
        return rc(sslots.at[owner], sslots.at[owner], gs_s.at[other], gs_r.at[owner], other, f)

    def s_send(i, carry):
        s_copy(s, (s + i) % seqs).start()
        return carry

    def s_recv(i, carry):
        s_copy((s + i) % seqs, (s + i) % seqs).wait_recv()
        return carry

    def s_done(i, carry):
        s_copy(s, (s + i) % seqs).wait_send()
        return carry

    lax.fori_loop(1, seqs, s_send, 0)
    lax.fori_loop(1, seqs, s_recv, 0)
    total = jnp.sum(sslots[...], axis=0)
    sum1_ref[...] = total[:, :chans]
    sum2_ref[...] = total[:, chans:]

    lax.fori_loop(1, seqs, s_done, 0)
    for i in range(1, 4):
        f_copy(f, (f + i) % 4).wait_send()
    for j in range(steps):
        y_copy(j, f).wait_send()
        z_send(j).wait_send()
        a_copy(j, far).wait_send()
        b_copy(j, far).wait_send()
    for u in range(UNITS):
        own_copy(u, f).wait_send()
    for k in range(3):
        swap(k, q).wait_send()
    pl.when(p < last)(lambda: fwd_next.wait_send())
    pl.when(p > 0)(lambda: fwd_prev.wait_send())
    for g in range(GROUPS):
        pl.when(p < last)(lambda: bwd_next(g).wait_send())
        pl.when(p > 0)(lambda: bwd_prev(g).wait_send())
    out_own.wait()
    for i in range(per):
        out_mate(i, q).wait_send()
        out_mate(i, 1 - q).wait_recv()


def body(block_input, dilated_weight, w_project, gain_first, gain_second, grad_output):
    seqs = lax.axis_size("seq")
    fsdps = lax.axis_size("fsdp")
    samples, bins, chans = block_input.shape
    hid = w_project.shape[0] * fsdps
    rows = 2 * bins
    bf16, f32 = jnp.bfloat16, jnp.float32
    dma = lambda n: pltpu.SemaphoreType.DMA((n,))
    steps = UNITS * CHUNKS
    anywhere = pl.BlockSpec(memory_space=pl.ANY)
    hbm = pl.BlockSpec(memory_space=pltpu.HBM)
    vmem = pl.BlockSpec(memory_space=pltpu.VMEM)
    out, sum1, sum2 = pl.pallas_call(
        functools.partial(kernel, seqs),
        out_shape=(
            jax.ShapeDtypeStruct(block_input.shape, bf16),
            jax.ShapeDtypeStruct((1, chans), f32),
            jax.ShapeDtypeStruct((1, hid), f32),
        ),
        in_specs=[hbm, hbm, hbm, vmem, vmem, hbm],
        out_specs=(anywhere, vmem, vmem),
        scratch_shapes=[
            pltpu.VMEM((2, bins, chans), bf16),
            pltpu.VMEM((2, bins, chans), bf16),
            pltpu.VMEM((3, chans, hid), bf16),
            pltpu.VMEM((hid, chans), bf16),
            pltpu.VMEM((rows, chans), bf16),
            pltpu.VMEM((rows, chans), f32),
            pltpu.VMEM((rows, chans), f32),
            pltpu.VMEM((rows, 128), f32),
            pltpu.VMEM((rows, hid), f32),
            pltpu.VMEM((rows, hid), f32),
            pltpu.VMEM((rows, hid), f32),
            pltpu.VMEM((rows, 128), f32),
            pltpu.VMEM((2, bins, hid), bf16),
            pltpu.VMEM((2, bins, hid), bf16),
            pltpu.VMEM((GROUPS, 2 * rows // GROUPS, hid), bf16),
            pltpu.VMEM((rows // GROUPS, chans), f32),
            pltpu.VMEM((chans, rows // GROUPS), f32),
            pltpu.VMEM((hid, rows), f32),
            pltpu.VMEM((2, bins, chans), bf16),
            pltpu.VMEM((8, chans), f32),
            pltpu.VMEM((8, hid), f32),
            pltpu.VMEM((fsdps, 1, chans + hid), f32),
            pltpu.VMEM((seqs, 1, chans + hid), f32),
        ]
        + [dma(steps)] * 8
        + [dma(UNITS)] * 3
        + [dma(3)] * 2
        + [dma(2)] * 3
        + [dma(2 * GROUPS)] * 2
        + [dma(bins // 32)] * 2
        + [dma(1)]
        + [dma(fsdps)] * 2
        + [dma(seqs)] * 2,
        compiler_params=pltpu.CompilerParams(
            collective_id=0, has_side_effects=True, vmem_limit_bytes=52 * 1024 * 1024
        ),
    )(
        block_input, dilated_weight, w_project,
        gain_first.reshape(1, chans), gain_second.reshape(1, hid), grad_output,
    )
    return out, sum1.reshape(chans), sum2.reshape(hid)


def solution(mesh):
    in_specs = (
        P("fsdp", "seq", None),
        P(None, "fsdp", None),
        P("fsdp", None),
        P(),
        P(),
        P("fsdp", "seq", None),
    )
    out_specs = (P("fsdp", "seq", None), P(), P())
    return jax.shard_map(body, mesh=mesh, in_specs=in_specs, out_specs=out_specs, check_vma=False)
```

```python
import functools

import jax
import jax.numpy as jnp
from jax import lax
from jax.experimental import pallas as pl
from jax.experimental.pallas import tpu as pltpu
from jax.sharding import PartitionSpec as P

MESH = pl.DeviceIdType.MESH
TAPS = (0, 2, 1)
GROUPS = 2
CHUNKS = 3
LAG = 2
AHEAD = 5
UNITS = 4
EPS = 1e-05
K0 = 0.7978845608028654
K1 = 0.044715


def normed(values):
    centre = values - jnp.mean(values, axis=-1, keepdims=True)
    scale = lax.rsqrt(jnp.mean(centre * centre, axis=-1, keepdims=True) + EPS)
    return centre * scale, scale


def gelu_parts(a):
    square = a * a
    t = jnp.tanh(a * (K0 + (K0 * K1) * square))
    half = 0.5 + 0.5 * t
    slope = half + (0.5 * a) * (1.0 - t * t) * (K0 + (3.0 * K0 * K1) * square)
    return a * half, slope


def dot(a, b):
    return jnp.dot(a, b, preferred_element_type=jnp.float32)


def dot_t(a, b):
    return lax.dot_general(a, b, (((1,), (1,)), ((), ())), preferred_element_type=jnp.float32)


def fold(values):
    rows, columns = values.shape
    return jnp.sum(values.reshape(rows // 8, 8, columns), axis=0)


def kernel(
    seqs, x_ref, w_ref, p_ref, g1_ref, g2_ref, go_ref,
    out_ref, sum1_ref, sum2_ref,
    xbuf, gbuf, wbuf, pbuf, hbuf, n1, q1, r1, acc, n2, q2, r2, psend, rfwd, gmx, gh, ght, g2t, obuf,
    part1, part2, fslots, sslots,
    y_s, y_r, z_s, z_r, a_s, a_r, b_s, b_r, own_s, own_r, own_l,
    sw_s, sw_r, sw_l, fw_s, fw_r, bw_s, bw_r, o_s, o_r, o_l, gf_s, gf_r, gs_s, gs_r,
):
    bins, chans = xbuf.shape[1], xbuf.shape[2]
    hid = pbuf.shape[0]
    wrows, prows = w_ref.shape[1], p_ref.shape[0]
    s, f = lax.axis_index("seq"), lax.axis_index("fsdp")
    reach = seqs // 8
    block = s // reach
    p, q = block // 2, block % 2
    zp = p % 2
    mate = s + reach - 2 * reach * q
    zmate = s + 2 * reach - 4 * reach * zp
    nxt, prv = s + 2 * reach, s - 2 * reach
    sib = f + 1 - 2 * (f % 2)
    far = (f + 2) % 4
    far_sib = (sib + 2) % 4

    def rc(src, dst, ss, rs, seq, fs):
        return pltpu.make_async_remote_copy(
            src_ref=src, dst_ref=dst, send_sem=ss, recv_sem=rs,
            device_id=(seq, fs), device_id_type=MESH,
        )

    barrier = pltpu.get_barrier_semaphore()

    def greet(i, carry):
        pl.semaphore_signal(barrier, inc=1, device_id=((s + i) % seqs, f), device_id_type=MESH)
        return carry

    lax.fori_loop(1, seqs, greet, 0)
    for i in range(1, 4):
        pl.semaphore_signal(barrier, inc=1, device_id=(s, (f + i) % 4), device_id_type=MESH)
    pl.semaphore_wait(barrier, seqs - 1 + 3)

    def held(u, owner, half, c):
        if u < 3:
            n = wrows // 2 // CHUNKS
            at = pl.multiple_of(owner * wrows + half * (wrows // 2) + c * n, 16)
            return wbuf.at[TAPS[u], pl.ds(at, n)]
        n = prows // 2 // CHUNKS
        at = pl.multiple_of(owner * prows + half * (prows // 2) + c * n, 16)
        return pbuf.at[pl.ds(at, n)]

    def mine(u, half, c):
        if u < 3:
            n = wrows // 2 // CHUNKS
            return w_ref.at[TAPS[u], pl.ds(pl.multiple_of(half * (wrows // 2) + c * n, 16), n)]
        n = prows // 2 // CHUNKS
        return p_ref.at[pl.ds(pl.multiple_of(half * (prows // 2) + c * n, 16), n)]

    def held_unit(u, owner):
        if u < 3:
            return wbuf.at[TAPS[u], pl.ds(pl.multiple_of(owner * wrows, 16), wrows)]
        return pbuf.at[pl.ds(pl.multiple_of(owner * prows, 16), prows)]

    def my_unit(u):
        return w_ref.at[TAPS[u]] if u < 3 else p_ref

    def route(j):
        if j >= CHUNKS and j % CHUNKS == CHUNKS - 1:
            return q, mate
        return zp, zmate

    def y_copy(j, owner):
        u, c = j // CHUNKS, j % CHUNKS
        half, unused = route(j)
        return rc(mine(u, half, c), held(u, owner, half, c), y_s.at[j], y_r.at[j], s, far)

    def z_send(j):
        half, partner = route(j)
        piece = held(j // CHUNKS, far, half, j % CHUNKS)
        return rc(piece, piece, z_s.at[j], z_r.at[j], partner, f)

    def z_recv(j):
        half, partner = route(j)
        piece = held(j // CHUNKS, far, 1 - half, j % CHUNKS)
        return rc(piece, piece, z_s.at[j], z_r.at[j], partner, f)

    def a_copy(j, owner):
        piece = held(j // CHUNKS, owner, route(j)[0], j % CHUNKS)
        return rc(piece, piece, a_s.at[j], a_r.at[j], s, sib)

    def b_copy(j, owner):
        piece = held(j // CHUNKS, owner, 1 - route(j)[0], j % CHUNKS)
        return rc(piece, piece, b_s.at[j], b_r.at[j], s, sib)

    def own_copy(u, owner):
        return rc(my_unit(u), held_unit(u, owner), own_s.at[u], own_r.at[u], s, sib)

    def own_local(u):
        return pltpu.make_async_copy(my_unit(u), held_unit(u, f), own_l.at[u])

    def swap(k, slot):
        if k == 0:
            return rc(x_ref.at[1 - q], xbuf.at[slot], sw_s.at[0], sw_r.at[0], mate, f)
        rows = pl.ds((k - 1) * (bins // 2), bins // 2)
        return rc(go_ref.at[1 - q, rows], gbuf.at[slot, rows], sw_s.at[k], sw_r.at[k], mate, f)

    def swap_local(k):
        ref, buf = ((x_ref, xbuf), (go_ref, gbuf))[k]
        return pltpu.make_async_copy(ref.at[q], buf.at[q], sw_l.at[k])

    steps = UNITS * CHUNKS
    swap_local(0).start()
    swap(0, q).start()
    for j in range(AHEAD):
        y_copy(j, f).start()
    for u in range(UNITS):
        own_copy(u, f).start()
        own_local(u).start()
    swap_local(1).start()

    tile = 32
    per = bins // tile

    def first_act(which):
        def go(i, carry):
            at = pl.multiple_of(which * bins + i * tile, tile)
            rows = pl.ds(at, tile)
            v = xbuf[which, pl.ds(pl.multiple_of(i * tile, tile), tile), :].astype(jnp.float32)
            n, scale = normed(v)
            act, slope = gelu_parts(n * g1_ref[...])
            hbuf[rows, :] = act.astype(jnp.bfloat16)
            n1[rows, :] = n
            q1[rows, :] = slope
            r1[rows, :] = jnp.broadcast_to(scale, (tile, 128))
            return carry

        lax.fori_loop(0, per, go, 0)

    def pump(j):
        if j < steps:
            y_copy(j, far).wait_recv()
            z_send(j).start()
            if j + AHEAD < steps:
                y_copy(j + AHEAD, f).start()
            a_copy(j, far).start()
        if j >= LAG:
            z_recv(j - LAG).wait_recv()
            b_copy(j - LAG, far).start()

    def near_ready(u):
        own_local(u).wait()
        own_copy(u, sib).wait_recv()

    def unit_ready(u):
        for c in range(CHUNKS):
            a_copy(u * CHUNKS + c, far_sib).wait_recv()
            b_copy(u * CHUNKS + c, far_sib).wait_recv()

    side = f // 2

    def span(which, size):
        return pl.ds(pl.multiple_of(which * size, 128), size)

    def fwd(k, which):
        rows = span(which, 2 * wrows)
        return dot(hbuf[:, rows], wbuf[k, rows, :])

    swap_local(0).wait()
    first_act(q)
    pump(0)
    pump(1)
    pump(2)
    pump(3)
    swap(0, 1 - q).wait_recv()
    first_act(1 - q)
    pump(4)
    near_ready(0)
    n2[...] = fwd(0, side)
    near_ready(1)
    q2[...] = fwd(2, side)
    near_ready(2)
    acc[...] = fwd(1, side)
    unit_ready(0)
    swap(1, q).start()

    n2[...] += fwd(0, 1 - side)
    acc[bins:, :] += n2[:bins, :]
    psend[0] = n2[bins:, :].astype(jnp.bfloat16)
    last = seqs // (2 * reach) - 1

    def to_next(src, dst, ss, rs):
        return rc(src, dst, ss, rs, nxt, f)

    def to_prev(src, dst, ss, rs):
        return rc(src, dst, ss, rs, prv, f)

    fwd_next = to_next(psend.at[0], rfwd.at[0], fw_s.at[0], fw_r.at[0])
    fwd_prev = to_prev(psend.at[1], rfwd.at[1], fw_s.at[1], fw_r.at[1])
    pl.when(p < last)(lambda: fwd_next.start())
    pump(5)
    pump(6)
    pump(7)
    unit_ready(1)
    swap(2, q).start()
    q2[...] += fwd(2, 1 - side)
    acc[:bins, :] += q2[bins:, :]
    psend[1] = q2[:bins, :].astype(jnp.bfloat16)
    pl.when(p > 0)(lambda: fwd_prev.start())
    pump(8)
    pump(9)
    pump(10)
    pump(11)
    unit_ready(2)
    acc[...] += fwd(1, 1 - side)

    part = bins // GROUPS

    def zero_first():
        rfwd[0] = jnp.zeros_like(rfwd[0])
        gmx[:, :part, :] = jnp.zeros((GROUPS, part, hid), jnp.bfloat16)

    def zero_last():
        rfwd[1] = jnp.zeros_like(rfwd[1])
        gmx[:, 3 * part:, :] = jnp.zeros((GROUPS, part, hid), jnp.bfloat16)

    pl.when(p == 0)(zero_first)
    pl.when(p == last)(zero_last)
    pl.when(p > 0)(lambda: fwd_next.wait_recv())
    pl.when(p < last)(lambda: fwd_prev.wait_recv())

    def second_act(i, carry):
        for which in range(2):
            rows = pl.ds(pl.multiple_of(which * bins + i * tile, tile), tile)
            got = rfwd[which, pl.ds(pl.multiple_of(i * tile, tile), tile), :]
            v = (acc[rows, :] + got.astype(jnp.float32)).astype(jnp.bfloat16).astype(jnp.float32)
            n, scale = normed(v)
            unused, slope = gelu_parts(n * g2_ref[...])
            n2[rows, :] = n
            q2[rows, :] = slope
            r2[rows, :] = jnp.broadcast_to(scale, (tile, 128))
        return carry

    lax.fori_loop(0, per, second_act, 0)
    pump(12)
    swap_local(1).wait()
    swap(1, 1 - q).wait_recv()
    swap(2, 1 - q).wait_recv()
    near_ready(3)

    def grad_hidden2(which):
        rows = span(which, 2 * prows)
        g2t[rows, :] = dot_t(pbuf[rows, :], gbuf[...].reshape(2 * bins, chans))

    grad_hidden2(side)
    pump(13)
    unit_ready(3)
    grad_hidden2(1 - side)

    def back(rows, d, n, slope, r, gain, total):
        da = d * slope
        total[...] += fold(da * n)
        dn = da * gain
        m1 = jnp.mean(dn, axis=-1, keepdims=True)
        m2 = jnp.mean(dn * n, axis=-1, keepdims=True)
        return r[rows, 0:1] * (dn - m1 - n * m2)

    part1[...] = jnp.zeros_like(part1)
    part2[...] = jnp.zeros_like(part2)

    for i in range(2):
        acc[i * bins:(i + 1) * bins, :] = g2t[:, i * bins:(i + 1) * bins].T
    each = part // tile

    def second_back(g, which):
        def go(i, carry):
            at = g * part + i * tile
            rows = pl.ds(pl.multiple_of(which * bins + at, tile), tile)
            dv = back(rows, acc[rows, :], n2[rows, :], q2[rows, :], r2, g2_ref[...], part2)
            to = pl.ds(pl.multiple_of((1 + which) * part + i * tile, tile), tile)
            gmx[g, to, :] = dv.astype(jnp.bfloat16)
            return carry

        lax.fori_loop(0, each, go, 0)

    def bwd_next(g):
        src, dst = gmx.at[g, pl.ds(2 * part, part)], gmx.at[g, pl.ds(0, part)]
        return to_next(src, dst, bw_s.at[2 * g], bw_r.at[2 * g])

    def bwd_prev(g):
        src, dst = gmx.at[g, pl.ds(part, part)], gmx.at[g, pl.ds(3 * part, part)]
        return to_prev(src, dst, bw_s.at[2 * g + 1], bw_r.at[2 * g + 1])

    for g in range(GROUPS):
        second_back(g, 1)
        pl.when(p < last)(lambda: bwd_next(g).start())
        second_back(g, 0)
        pl.when(p > 0)(lambda: bwd_prev(g).start())

    def out_mate(i, which):
        rows = pl.ds(pl.multiple_of(i * tile, tile), tile)
        return rc(obuf.at[1 - q, rows], out_ref.at[which, rows], o_s.at[i], o_r.at[i], mate, f)

    def first_back(g, which, send):
        def go(i, carry):
            rows = pl.ds(pl.multiple_of(which * part + i * tile, tile), tile)
            at = g * part + i * tile
            all_rows = pl.ds(pl.multiple_of(which * bins + at, tile), tile)
            here = pl.ds(pl.multiple_of(at, tile), tile)
            dv = back(all_rows, gh[rows, :], n1[all_rows, :], q1[all_rows, :], r1, g1_ref[...], part1)
            obuf[which, here, :] = (gbuf[which, here, :].astype(jnp.float32) + dv).astype(jnp.bfloat16)
            if send:
                out_mate(g * each + i, q).start()
            return carry

        lax.fori_loop(0, each, go, 0)

    for g in range(GROUPS):
        ght[...] = dot_t(wbuf[1], gmx[g, part:3 * part, :])
        pl.when(p > 0)(lambda: bwd_next(g).wait_recv())
        pl.when(p < last)(lambda: bwd_prev(g).wait_recv())
        ght[...] += dot_t(wbuf[0], gmx[g, 2 * part:, :])
        ght[...] += dot_t(wbuf[2], gmx[g, :2 * part, :])
        gh[...] = ght[...].T
        first_back(g, 1 - q, True)
        first_back(g, q, False)
    out_own = pltpu.make_async_copy(obuf.at[q], out_ref.at[q], o_l.at[0])
    out_own.start()

    fslots[f, :, :chans] = jnp.sum(part1[...], axis=0, keepdims=True)
    fslots[f, :, chans:] = jnp.sum(part2[...], axis=0, keepdims=True)

    def f_copy(owner, other):
        return rc(fslots.at[owner], fslots.at[owner], gf_s.at[other], gf_r.at[owner], s, other)

    for i in range(1, 4):
        f_copy(f, (f + i) % 4).start()
    for i in range(1, 4):
        f_copy((f + i) % 4, (f + i) % 4).wait_recv()
    sslots[s] = jnp.sum(fslots[...], axis=0)

    def s_copy(owner, other):
        return rc(sslots.at[owner], sslots.at[owner], gs_s.at[other], gs_r.at[owner], other, f)

    def s_send(i, carry):
        s_copy(s, (s + i) % seqs).start()
        return carry

    def s_recv(i, carry):
        s_copy((s + i) % seqs, (s + i) % seqs).wait_recv()
        return carry

    def s_done(i, carry):
        s_copy(s, (s + i) % seqs).wait_send()
        return carry

    lax.fori_loop(1, seqs, s_send, 0)
    lax.fori_loop(1, seqs, s_recv, 0)
    total = jnp.sum(sslots[...], axis=0)
    sum1_ref[...] = total[:, :chans]
    sum2_ref[...] = total[:, chans:]

    lax.fori_loop(1, seqs, s_done, 0)
    for i in range(1, 4):
        f_copy(f, (f + i) % 4).wait_send()
    for j in range(steps):
        y_copy(j, f).wait_send()
        z_send(j).wait_send()
        a_copy(j, far).wait_send()
        b_copy(j, far).wait_send()
    for u in range(UNITS):
        own_copy(u, f).wait_send()
    for k in range(3):
        swap(k, q).wait_send()
    pl.when(p < last)(lambda: fwd_next.wait_send())
    pl.when(p > 0)(lambda: fwd_prev.wait_send())
    for g in range(GROUPS):
        pl.when(p < last)(lambda: bwd_next(g).wait_send())
        pl.when(p > 0)(lambda: bwd_prev(g).wait_send())
    out_own.wait()
    for i in range(per):
        out_mate(i, q).wait_send()
        out_mate(i, 1 - q).wait_recv()


def body(block_input, dilated_weight, w_project, gain_first, gain_second, grad_output):
    seqs = lax.axis_size("seq")
    fsdps = lax.axis_size("fsdp")
    samples, bins, chans = block_input.shape
    hid = w_project.shape[0] * fsdps
    rows = 2 * bins
    bf16, f32 = jnp.bfloat16, jnp.float32
    dma = lambda n: pltpu.SemaphoreType.DMA((n,))
    steps = UNITS * CHUNKS
    anywhere = pl.BlockSpec(memory_space=pl.ANY)
    hbm = pl.BlockSpec(memory_space=pltpu.HBM)
    vmem = pl.BlockSpec(memory_space=pltpu.VMEM)
    out, sum1, sum2 = pl.pallas_call(
        functools.partial(kernel, seqs),
        out_shape=(
            jax.ShapeDtypeStruct(block_input.shape, bf16),
            jax.ShapeDtypeStruct((1, chans), f32),
            jax.ShapeDtypeStruct((1, hid), f32),
        ),
        in_specs=[hbm, hbm, hbm, vmem, vmem, hbm],
        out_specs=(anywhere, vmem, vmem),
        scratch_shapes=[
            pltpu.VMEM((2, bins, chans), bf16),
            pltpu.VMEM((2, bins, chans), bf16),
            pltpu.VMEM((3, chans, hid), bf16),
            pltpu.VMEM((hid, chans), bf16),
            pltpu.VMEM((rows, chans), bf16),
            pltpu.VMEM((rows, chans), f32),
            pltpu.VMEM((rows, chans), f32),
            pltpu.VMEM((rows, 128), f32),
            pltpu.VMEM((rows, hid), f32),
            pltpu.VMEM((rows, hid), f32),
            pltpu.VMEM((rows, hid), f32),
            pltpu.VMEM((rows, 128), f32),
            pltpu.VMEM((2, bins, hid), bf16),
            pltpu.VMEM((2, bins, hid), bf16),
            pltpu.VMEM((GROUPS, 2 * rows // GROUPS, hid), bf16),
            pltpu.VMEM((rows // GROUPS, chans), f32),
            pltpu.VMEM((chans, rows // GROUPS), f32),
            pltpu.VMEM((hid, rows), f32),
            pltpu.VMEM((2, bins, chans), bf16),
            pltpu.VMEM((8, chans), f32),
            pltpu.VMEM((8, hid), f32),
            pltpu.VMEM((fsdps, 1, chans + hid), f32),
            pltpu.VMEM((seqs, 1, chans + hid), f32),
        ]
        + [dma(steps)] * 8
        + [dma(UNITS)] * 3
        + [dma(3)] * 2
        + [dma(2)] * 3
        + [dma(2 * GROUPS)] * 2
        + [dma(bins // 32)] * 2
        + [dma(1)]
        + [dma(fsdps)] * 2
        + [dma(seqs)] * 2,
        compiler_params=pltpu.CompilerParams(
            collective_id=0, has_side_effects=True, vmem_limit_bytes=52 * 1024 * 1024
        ),
    )(
        block_input, dilated_weight, w_project,
        gain_first.reshape(1, chans), gain_second.reshape(1, hid), grad_output,
    )
    return out, sum1.reshape(chans), sum2.reshape(hid)


def solution(mesh):
    in_specs = (
        P("fsdp", "seq", None),
        P(None, "fsdp", None),
        P("fsdp", None),
        P(),
        P(),
        P("fsdp", "seq", None),
    )
    out_specs = (P("fsdp", "seq", None), P(), P())
    return jax.shard_map(body, mesh=mesh, in_specs=in_specs, out_specs=out_specs, check_vma=False)
```
